256 devices in a mesh: blk: 128 (over z, y_hi, x, core), feat: 2 (over y_lo).
Axes of the slice: x: 4, y: 4 (y_hi: 2, y_lo: 2; y = y_hi * 2 + y_lo), z: 8, core: 2. Of those that a mesh axis runs over, the one named last changes fastest.
Arguments:
- images: bfloat16 [131072, 1152], P('blk', 'feat'), may hold values from -1 to 1
- texts: bfloat16 [2048, 1152], P('blk', 'feat'), may hold values from -1 to 1
- img_group: int32 [1024], replicated, may hold values from 0 to 31
- txt_group: int32 [16], replicated, may hold values from 0 to 31
- temp: float32 [], replicated, may hold values from 2 to 4
- bias: float32 [], replicated, may hold values from -3 to -1
- loss_scale: float32 [], replicated, may hold values from 16384 to 65536
Outputs:
- grad_images: float32 [131072, 1152], P('blk', 'feat')
- grad_texts: float32 [2048, 1152], P('blk', 'feat')
The draws below stay inside these ranges and needn't reach their ends.
All inputs are finite; a program needn't handle non-finite values.
Results may differ from the reference program's by a relative error of at most 0.0023.
Values may be sent and summed in bfloat16 or wider, within the bound.
A program may use at most 64 MiB of HBM per device.

```python
import math
import jax
import jax.numpy as jnp
from jax import lax

D = 1152
GROUPS = 32
IMAGES = 131072
TEXTS = 2048


def touch_ends(drawn, rng, smallest, largest):
    shape = drawn.shape
    index_at = [jax.random.randint(jax.random.fold_in(rng, axis), (), 0, shape[axis]) for axis in range(len(shape))]
    drawn = drawn.at[tuple(index_at)].set(smallest)
    longest = shape.index(max(shape))
    index_at[longest] = (index_at[longest] + 1) % shape[longest]
    return drawn.at[tuple(index_at)].set(largest)


def block_scale(key, dims, cuts, low, high):
    def one(position, blocks):
        draws = jax.random.uniform(jax.random.fold_in(jax.random.fold_in(key, 6), position), (blocks,), jnp.float32, low / len(cuts), high / len(cuts))
        return jnp.repeat(jnp.exp(draws), dims[position] // blocks).reshape((-1,) + (1,) * (len(dims) - position - 1))

    gain = one(*cuts[0])
    for cut in cuts[1:]:
        gain = gain * one(*cut)
    return gain


def centred(key, dims, deviation, reach, pieces=(), dtype=jnp.bfloat16):
    factor_of = block_scale(key, dims, pieces, -0.22, 0.18) if pieces else 1.0
    values = jax.random.normal(key, dims, jnp.float32) * deviation * factor_of
    return jnp.minimum(jnp.maximum(values, -reach), reach).astype(dtype)


def setup_inputs(seed: int = 0) -> dict:
    arg_keys = jax.random.split(jax.random.key(seed), 8)
    return {
        "images": centred(arg_keys[0], (IMAGES, D), (D ** -0.25), 1.0, ((0, 128), (1, 2))),
        "texts": centred(arg_keys[1], (TEXTS, D), (D ** -0.25), 1.0, ((0, 128), (1, 2))),
        "img_group": touch_ends(jax.random.randint(arg_keys[2], (IMAGES // 128,), 0, GROUPS), jax.random.fold_in(arg_keys[2], 1), 0, GROUPS - 1).astype(jnp.int32),
        "txt_group": touch_ends(jax.random.randint(arg_keys[3], (TEXTS // 128,), 0, GROUPS), jax.random.fold_in(arg_keys[3], 1), 0, GROUPS - 1).astype(jnp.int32),
        "temp": jnp.clip(jax.random.uniform(arg_keys[4], (), jnp.float32, 2.0, 4.0), 2.0, 4.0),
        "bias": jnp.clip(jax.random.uniform(arg_keys[5], (), jnp.float32, -3.0, -1.0), -3.0, -1.0),
        "loss_scale": jnp.clip(jnp.exp(jax.random.uniform(arg_keys[6], (), jnp.float32, math.log(16384.0), math.log(65536.0))), 16384.0, 65536.0),
    }


def reference(images, texts, img_group, txt_group, temp, bias, loss_scale):
    total_images = images.shape[0]
    width = images.shape[1]
    col_group = jnp.repeat(img_group, 128)
    factor = -(loss_scale * temp / total_images)
    text_blocks = texts.reshape(-1, 128, width)

    def one_block(grad_acc, item):
        block, group = item
        logits = temp * jnp.dot(block, images.T, preferred_element_type=jnp.float32) + bias
        sign = jnp.where(col_group[None, :] == group, 1.0, -1.0).astype(jnp.float32)
        weights = (factor * sign * jax.nn.sigmoid(-sign * logits)).astype(jnp.bfloat16)
        grad_text = jnp.dot(weights, images, preferred_element_type=jnp.float32)
        grad_acc = grad_acc + jnp.dot(weights.T, block, preferred_element_type=jnp.float32)
        return grad_acc, grad_text

    start = jnp.zeros((total_images, width), jnp.float32)
    grad_images, grad_texts = lax.scan(one_block, start, (text_blocks, txt_group))
    return grad_images, grad_texts.reshape(-1, width)
```

```python
import functools

import jax
import jax.numpy as jnp
from jax import lax
from jax.experimental import pallas as pl
from jax.experimental.pallas import tpu as pltpu
from jax.sharding import PartitionSpec as P

MESH = pl.DeviceIdType.MESH
NZ, NY, NX = 8, 2, 4
R = 16
CH = 256


def chain_lengths(n):
    return n // 2, (n - 1) // 2


def kernel(
    cfg,
    img_ref, txt_ref, ig_ref, tg_ref, temp_ref, bias_ref, scale_ref,
    gi_out, gt_out,
    T, TT, I, W, G, gI, gIr, tgv, tp,
    rAzf, rAzb, rAxf, rAxb, rBxf, rBxb, rBzf, rBzb, rY, finY,
    send, recv, loc,
):
    nz, ny, nx, F, FP, C, total_images = cfg
    HALF = nz * nx * R
    ROWS = 2 * HALF
    NCH = C // CH
    blk = lax.axis_index("blk")
    feat = lax.axis_index("feat")
    core = lax.rem(blk, 2)
    x = lax.rem(blk // 2, nx)
    yh = lax.rem(blk // (2 * nx), ny)
    z = blk // (2 * nx * ny)
    step_dir = 1 - 2 * core

    def at(z_, yh_, x_, core_, feat_):
        return (((z_ * ny + yh_) * nx + x_) * 2 + core_, feat_)

    def zz(k):
        return lax.rem(z + step_dir * k + 2 * nz, nz)

    def xx(k):
        return lax.rem(x + step_dir * k + 2 * nx, nx)

    sibling = at(z, yh, x, 1 - core, feat)
    dev_f = at(z, yh, x, core, 1 - feat)
    dev_y = at(z, 1 - yh, x, core, feat)
    dev_d = at(z, 1 - yh, x, core, 1 - feat)
    zf, zb = at(zz(1), yh, x, core, feat), at(zz(-1), yh, x, core, feat)
    xf, xb = at(z, yh, xx(1), core, feat), at(z, yh, xx(-1), core, feat)

    barrier = pltpu.get_barrier_semaphore()
    partners = (sibling, dev_f, dev_y, dev_d, zf, zb, xf, xb)
    for dev in partners:
        pl.semaphore_signal(barrier, inc=1, device_id=dev, device_id_type=MESH)
    pl.semaphore_wait(barrier, len(partners))

    count = [0]
    started = []

    def copy_to(src, dst, dev):
        i = count[0]
        count[0] += 1
        c = pltpu.make_async_remote_copy(
            src_ref=src, dst_ref=dst, send_sem=send.at[i], recv_sem=recv.at[i], device_id=dev, device_id_type=MESH
        )
        c.start()
        started.append(c)
        return c

    tp[...] = jnp.zeros_like(tp)
    tp[:, 0:F] = txt_ref[...]

    def rowsA(z_, x_):
        return pl.multiple_of((z_ * nx + x_) * R, R)

    def rowsB(z_, x_):
        return pl.multiple_of(HALF + (x_ * nz + z_) * R, R)

    myrow = pl.multiple_of(jnp.where(yh == 0, rowsA(z, x), rowsB(z, x)), R)
    mylane = pl.multiple_of(feat * FP, 128)
    T[pl.ds(myrow, R), pl.ds(mylane, FP)] = tp[...]
    own_dst = T.at[pl.ds(myrow, R), pl.ds(mylane, FP)]
    y_copies = [copy_to(tp, own_dst, dev) for dev in (dev_f, dev_y, dev_d)]

    frow = pl.multiple_of(feat * FP, 16)
    orow = pl.multiple_of((1 - feat) * FP, 16)
    img_copies = []
    for j in range(NCH):
        cols = pl.ds(j * CH, CH)
        img_copies.append(copy_to(img_ref.at[:, cols], I.at[core, pl.ds(frow, F), cols], dev_f))
    sib_own = copy_to(img_ref, I.at[core, pl.ds(frow, F), :], sibling)
    own_copy = pltpu.make_async_copy(img_ref, I.at[core, pl.ds(frow, F), :], loc.at[0])
    own_copy.start()

    for r in range(2):
        for f in range(2):
            I[r, f * FP + F : (f + 1) * FP, :] = jnp.zeros((FP - F, C), jnp.bfloat16)

    def fill_groups(i, carry):
        za, xb_ = i // nx, i // nz
        tgv[pl.ds(pl.multiple_of(i * R, R), R), :] = jnp.full((R, 128), tg_ref[za * ny], jnp.int32)
        zb_ = i - xb_ * nz
        tgv[pl.ds(pl.multiple_of(HALF + i * R, R), R), :] = jnp.full((R, 128), tg_ref[zb_ * ny + 1], jnp.int32)
        return carry

    lax.fori_loop(0, nz * nx, fill_groups, 0)

    def blockAx(k):
        return T.at[pl.ds(rowsA(z, xx(k)), R), :]

    def blockAz(k):
        return T.at[pl.ds(rowsA(zz(k), 0), nx * R), :]

    def blockBz(k):
        return T.at[pl.ds(rowsB(zz(k), x), R), :]

    def blockBx(k):
        return T.at[pl.ds(rowsB(0, xx(k)), nz * R), :]

    class Gather:
        def __init__(self, block, fwd, bwd, n):
            self.block, self.fwd, self.bwd = block, fwd, bwd
            self.lf, self.lb = chain_lengths(n)
            self.cf, self.cb = [], []

        def send(self, s):
            if s < self.lf:
                self.cf.append(copy_to(self.block(-s), self.block(-s), self.fwd))
            if s < self.lb:
                self.cb.append(copy_to(self.block(s), self.block(s), self.bwd))

        def wait(self, s):
            if s < self.lf:
                self.cf[s].wait_recv()
            if s < self.lb:
                self.cb[s].wait_recv()

    gAx, gAz = Gather(blockAx, xf, xb, nx), Gather(blockAz, zf, zb, nz)
    gBx, gBz = Gather(blockBx, xf, xb, nx), Gather(blockBz, zf, zb, nz)
    lx, lz = nx // 2, nz // 2

    for c in y_copies:
        c.wait_recv()
    gAx.send(0)
    gBz.send(0)
    for s in range(lx):
        gAx.wait(s)
        gAx.send(s + 1)
        gBz.wait(s)
        gBz.send(s + 1)
    gAz.send(0)
    for s in range(lx, lz):
        gBz.wait(s)
        gBz.send(s + 1)
    gBx.send(0)
    for s in range(lz):
        gAz.wait(s)
        gAz.send(s + 1)
        if s < lx:
            gBx.wait(s)
            gBx.send(s + 1)

    def transpose_rows(i, carry):
        rows = pl.ds(pl.multiple_of(i * 128, 128), 128)
        TT[:, rows] = T[rows, pl.ds(mylane, FP)].T
        return carry

    lax.fori_loop(0, ROWS // 128, transpose_rows, 0)

    own_copy.wait()
    sib_own.wait_recv()

    temp, bias = temp_ref[0], bias_ref[0]
    factor = -(scale_ref[0] * temp / total_images)
    base = count[0]
    count[0] += 2 * NCH
    TM = min(256, ROWS)
    FM = F // 3

    def fwd_copy(j):
        cols = pl.ds(pl.multiple_of(j * CH, CH), CH)
        ref = I.at[core, pl.ds(orow, F), cols]
        return pltpu.make_async_remote_copy(
            src_ref=ref, dst_ref=ref, send_sem=send.at[base + j], recv_sem=recv.at[base + j], device_id=sibling, device_id_type=MESH
        )

    def gi_copy(j):
        cols = pl.ds(pl.multiple_of(j * CH, CH), CH)
        return pltpu.make_async_remote_copy(
            src_ref=gI.at[1, :, cols], dst_ref=gIr.at[:, cols],
            send_sem=send.at[base + NCH + j], recv_sem=recv.at[base + NCH + j], device_id=sibling, device_id_type=MESH,
        )

    def img_wait(j):
        cols = pl.ds(pl.multiple_of(j * CH, CH), CH)
        return pltpu.make_async_remote_copy(
            src_ref=img_ref.at[:, cols], dst_ref=I.at[core, pl.ds(frow, F), cols],
            send_sem=send.at[3 + j], recv_sem=recv.at[3 + j], device_id=dev_f, device_id_type=MESH,
        )

    def step(k, carry):
        j = k // 2
        which = lax.rem(k, 2)
        r = jnp.where(which == 0, core, 1 - core)
        cols = pl.ds(pl.multiple_of(j * CH, CH), CH)

        @pl.when(which == 0)
        def _():
            img_wait(j).wait_recv()
            fwd_copy(j).start()

        @pl.when(which == 1)
        def _():
            fwd_copy(j).wait_recv()

        first_group = (blk - core + r) * (C // 128) + j * (CH // 128)

        def tile(m, carry2):
            rows = pl.ds(pl.multiple_of(m * TM, TM), TM)
            raw = jnp.dot(T[rows, :], I[r, :, cols], preferred_element_type=jnp.float32)
            tg = tgv[rows, :]
            for q in range(CH // 128):
                logit = temp * raw[:, q * 128 : (q + 1) * 128] + bias
                same = tg == ig_ref[first_group + q]
                p = 1.0 / (1.0 + jnp.exp(jnp.where(same, logit, -logit)))
                W[rows, q * 128 : (q + 1) * 128] = (jnp.where(same, factor, -factor) * p).astype(jnp.bfloat16)
            part = lax.dot_general(
                W[rows, :], I[r, pl.ds(frow, FP), cols], (((1,), (1,)), ((), ())), preferred_element_type=jnp.float32
            )

            @pl.when(k == 0)
            def _():
                G[rows, :] = part

            @pl.when(k != 0)
            def _():
                G[rows, :] = G[rows, :] + part

            return carry2

        lax.fori_loop(0, ROWS // TM, tile, 0)

        def gi_tile(m, carry2):
            rows = pl.ds(pl.multiple_of(m * FM, 16), FM)
            gI[which, rows, cols] = jnp.dot(TT[rows, :], W[...], preferred_element_type=jnp.float32)
            return carry2

        lax.fori_loop(0, 3, gi_tile, 0)

        @pl.when(which == 1)
        def _():
            gi_copy(j).start()

        return carry

    lax.fori_loop(0, 2 * NCH, step, 0)

    class Reduce:
        def __init__(self, block, rf, rb, fwd, bwd, n):
            self.block, self.rf, self.rb, self.fwd, self.bwd = block, rf, rb, fwd, bwd
            self.lf, self.lb = chain_lengths(n)
            self.cf, self.cb = [], []

        def send(self, s):
            if s < self.lf:
                src = self.block(self.lf - s)
                if s > 0:
                    self.rf[s - 1, :, :] = self.rf[s - 1] + src[...]
                    src = self.rf.at[s - 1]
                self.cf.append(copy_to(src, self.rf.at[s], self.fwd))
            if s < self.lb:
                src = self.block(-(self.lb - s))
                if s > 0:
                    self.rb[s - 1, :, :] = self.rb[s - 1] + src[...]
                    src = self.rb.at[s - 1]
                self.cb.append(copy_to(src, self.rb.at[s], self.bwd))

        def wait(self, s):
            if s < self.lf:
                self.cf[s].wait_recv()
            if s < self.lb:
                self.cb[s].wait_recv()

        def finish(self):
            total = self.rf[self.lf - 1] + self.block(0)[...]
            if self.lb:
                total = total + self.rb[self.lb - 1]
            self.rf[self.lf - 1, :, :] = total
            return self.rf.at[self.lf - 1]

    def rAz(k):
        return G.at[pl.ds(rowsA(zz(k), 0), nx * R), :]

    def rBx(k):
        return G.at[pl.ds(rowsB(0, xx(k)), nz * R), :]

    sAz = Reduce(rAz, rAzf, rAzb, zf, zb, nz)
    sBx = Reduce(rBx, rBxf, rBxb, xf, xb, nx)
    sAz.send(0)
    sBx.send(0)
    for s in range(lx):
        sAz.wait(s)
        sAz.send(s + 1)
        sBx.wait(s)
        sBx.send(s + 1)
    totB = sBx.finish()
    sBz = Reduce(lambda k: totB.at[pl.ds(pl.multiple_of(zz(k) * R, R), R), :], rBzf, rBzb, zf, zb, nz)
    sBz.send(0)

    out_copies = []
    for j in range(NCH):
        cols = pl.ds(j * CH, CH)
        gi_copy(j).wait_recv()
        gI[0, :, cols] = gI[0, :, cols] + gIr[:, cols]
        c = pltpu.make_async_copy(gI.at[0, :, cols], gi_out.at[:, cols], loc.at[1 + j])
        c.start()
        out_copies.append(c)

    for s in range(lx, lz):
        sAz.wait(s)
        sAz.send(s + 1)
        sBz.wait(s - lx)
        sBz.send(s - lx + 1)
    totA = sAz.finish()
    sAx = Reduce(lambda k: totA.at[pl.ds(pl.multiple_of(xx(k) * R, R), R), :], rAxf, rAxb, xf, xb, nx)
    sAx.send(0)
    for s in range(lx):
        sAx.wait(s)
        sAx.send(s + 1)
        sBz.wait(lz - lx + s)
        sBz.send(lz - lx + s + 1)
    endA, endB = sAx.finish(), sBz.finish()
    mineA = (yh == 0).astype(jnp.float32)
    a, b = endA[...], endB[...]
    finY[...] = b * mineA + a * (1.0 - mineA)
    last = copy_to(finY, rY, dev_y)
    own = a * mineA + b * (1.0 - mineA)
    last.wait_recv()
    gt_out[...] = (own + rY[...])[:, 0:F]

    for c in started:
        c.wait_send()
    for j in range(NCH):
        fwd_copy(j).wait_send()
        gi_copy(j).wait_send()
    for c in out_copies:
        c.wait()


def build(nz, ny, nx, F, FP, C, total_images):
    lfx, lbx = chain_lengths(nx)
    lfz, lbz = chain_lengths(nz)
    rows = 2 * nz * nx * R
    f32, bf16 = jnp.float32, jnp.bfloat16
    scratch = [
        pltpu.VMEM((rows, 2 * FP), bf16),
        pltpu.VMEM((FP, rows), bf16),
        pltpu.VMEM((2, 2 * FP, C), bf16),
        pltpu.VMEM((rows, CH), bf16),
        pltpu.VMEM((rows, FP), f32),
        pltpu.VMEM((2, F, C), f32),
        pltpu.VMEM((F, C), f32),
        pltpu.VMEM((rows, 128), jnp.int32),
        pltpu.VMEM((R, FP), bf16),
        pltpu.VMEM((lfz, nx * R, FP), f32),
        pltpu.VMEM((max(lbz, 1), nx * R, FP), f32),
        pltpu.VMEM((lfx, R, FP), f32),
        pltpu.VMEM((max(lbx, 1), R, FP), f32),
        pltpu.VMEM((lfx, nz * R, FP), f32),
        pltpu.VMEM((max(lbx, 1), nz * R, FP), f32),
        pltpu.VMEM((lfz, R, FP), f32),
        pltpu.VMEM((max(lbz, 1), R, FP), f32),
        pltpu.VMEM((R, FP), f32),
        pltpu.VMEM((R, FP), f32),
        pltpu.SemaphoreType.DMA((80,)),
        pltpu.SemaphoreType.DMA((80,)),
        pltpu.SemaphoreType.DMA((1 + C // CH,)),
    ]
    smem = pl.BlockSpec(memory_space=pltpu.SMEM)
    vmem = pl.BlockSpec(memory_space=pltpu.VMEM)
    hbm = pl.BlockSpec(memory_space=pl.ANY)

    def body(images, texts, img_group, txt_group, temp, bias, loss_scale):
        gi, gt = pl.pallas_call(
            functools.partial(kernel, (nz, ny, nx, F, FP, C, total_images)),
            out_shape=(jax.ShapeDtypeStruct((F, C), f32), jax.ShapeDtypeStruct((R, F), f32)),
            in_specs=[hbm, vmem, smem, smem, smem, smem, smem],
            out_specs=(hbm, vmem),
            scratch_shapes=scratch,
            compiler_params=pltpu.CompilerParams(
                collective_id=0, has_side_effects=True, vmem_limit_bytes=56 * 1024 * 1024
            ),
        )(images.T, texts, img_group, txt_group, temp.reshape(1), bias.reshape(1), loss_scale.reshape(1))
        return gi.T, gt

    return body


def solution(mesh):
    body = build(NZ, NY, NX, 576, 640, 1024, 131072)
    in_specs = (P("blk", "feat"), P("blk", "feat"), P(), P(), P(), P(), P())
    out_specs = (P("blk", "feat"), P("blk", "feat"))
    return jax.shard_map(body, mesh=mesh, in_specs=in_specs, out_specs=out_specs, check_vma=False)
```

```python
import functools

import jax
import jax.numpy as jnp
from jax import lax
from jax.experimental import pallas as pl
from jax.experimental.pallas import tpu as pltpu
from jax.sharding import PartitionSpec as P

MESH = pl.DeviceIdType.MESH
NZ, NY, NX = 8, 2, 4
R = 16
CH = 256
WIRE_A = jnp.float32
WIRE_B = jnp.float32


def chain_lengths(n):
    return n // 2, (n - 1) // 2


def near_first(n):
    lf, lb = chain_lengths(n)
    return sorted(range(-lf, lb + 1), key=lambda k: (abs(k), k))


def kernel(
    cfg,
    img_ref, txt_ref, ig_ref, tg_ref, temp_ref, bias_ref, scale_ref,
    gi_out, gt_out,
    T, TT, I, W, G, gI, gIr, tgv, Y,
    sAzf, sAzb, rAzf, rAzb, sBxf, sBxb, rBxf, rBxb,
    SA, rAx, SB, rBzf, rBzb, finY, rY,
    send, recv, loc,
):
    nz, ny, nx, F, C, total_images = cfg
    NCH = C // CH
    HZ = nz // 2
    TM = HZ * nx * R
    W2 = 2 * CH
    ZO, XO = near_first(nz), near_first(nx)
    lfz, lbz = chain_lengths(nz)
    lfx, lbx = chain_lengths(nx)

    def norm(k, n):
        return k - n if k > (n - 1) // 2 else k

    def zi(k):
        return ZO.index(norm(k, nz))

    def xi(k):
        return XO.index(norm(k, nx))

    blk = lax.axis_index("blk")
    feat = lax.axis_index("feat")
    core = lax.rem(blk, 2)
    x = lax.rem(blk // 2, nx)
    yh = lax.rem(blk // (2 * nx), ny)
    z = blk // (2 * nx * ny)
    step_dir = 1 - 2 * core

    def at(z_, yh_, x_, core_, feat_):
        return (((z_ * ny + yh_) * nx + x_) * 2 + core_, feat_)

    def zz(k):
        return lax.rem(z + step_dir * k + 2 * nz, nz)

    def xx(k):
        return lax.rem(x + step_dir * k + 2 * nx, nx)

    sibling = at(z, yh, x, 1 - core, feat)
    dev_f = at(z, yh, x, core, 1 - feat)
    dev_y = at(z, 1 - yh, x, core, feat)
    dev_d = at(z, 1 - yh, x, core, 1 - feat)
    zf, zb = at(zz(1), yh, x, core, feat), at(zz(-1), yh, x, core, feat)

    def xd(k):
        return at(z, yh, xx(k), core, feat)

    x_steps = [k for k in (1, -1, 2) if k < nx and (k != -1 or nx > 2)]
    barrier = pltpu.get_barrier_semaphore()
    partners = [sibling, dev_f, dev_y, dev_d, zf, zb] + [xd(k) for k in x_steps]
    for dev in partners:
        pl.semaphore_signal(barrier, inc=1, device_id=dev, device_id_type=MESH)

    ccol = pl.multiple_of(core * CH, 128)
    frow = pl.multiple_of(feat * F, 16)
    orow = pl.multiple_of((1 - feat) * F, 16)

    def img_src(j):
        return img_ref.at[:, pl.ds(j * CH, CH)]

    def img_dst(j):
        return I.at[j, pl.ds(frow, F), pl.ds(ccol, CH)]

    own_copies = [pltpu.make_async_copy(img_src(j), img_dst(j), loc.at[j]) for j in range(NCH)]
    for c in own_copies:
        c.start()
    me = yh * 2 + feat
    Y[me, :, 0:F] = txt_ref[...]
    for i, kz in enumerate(ZO):
        t, a = divmod(i, HZ)
        for h in range(2):
            group = jnp.full((nx * R, 128), tg_ref[zz(kz) * ny + h], jnp.int32)
            tgv[2 * h + t, a * nx * R : (a + 1) * nx * R, :] = group
    G[...] = jnp.zeros_like(G)

    pl.semaphore_wait(barrier, len(partners))

    count = [0]
    started = []

    def copy_to(src, dst, dev):
        i = count[0]
        count[0] += 1
        c = pltpu.make_async_remote_copy(
            src_ref=src, dst_ref=dst, send_sem=send.at[i], recv_sem=recv.at[i], device_id=dev, device_id_type=MESH
        )
        c.start()
        started.append(c)
        return c

    y_copies = [copy_to(Y.at[me], Y.at[me], dev) for dev in (dev_f, dev_y, dev_d)]
    img_copies = [copy_to(img_src(j), img_dst(j), dev_f) for j in range(NCH)]
    sib_copies = [copy_to(img_src(j), img_dst(j), sibling) for j in range(NCH)]
    fwd_copies = {}

    def forward_images(j):
        if j < NCH:
            img_copies[j].wait_recv()
            ref = I.at[j, pl.ds(orow, F), pl.ds(ccol, CH)]
            fwd_copies[j] = copy_to(ref, ref, sibling)

    ready = set()

    def images_ready(j):
        if j < NCH and j not in ready:
            ready.add(j)
            own_copies[j].wait()
            sib_copies[j].wait_recv()
            fwd_copies[j].wait_recv()

    temp, bias = temp_ref[0], bias_ref[0]
    factor = -(scale_ref[0] * temp / total_images)

    def task(m, j):
        raw = jnp.dot(T[m].reshape(TM, 2 * F), I[j], preferred_element_type=jnp.float32)
        tg = tgv[m]
        parts = []
        for q in range(W2 // 128):
            per = CH // 128
            group = ig_ref[(blk - core + q // per) * (C // 128) + j * per + q % per]
            logit = temp * raw[:, q * 128 : (q + 1) * 128] + bias
            same = tg == group
            p = 1.0 / (1.0 + jnp.exp(jnp.where(same, logit, -logit)))
            parts.append((jnp.where(same, factor, -factor) * p).astype(jnp.bfloat16))
        w = jnp.concatenate(parts, axis=1)
        W[j, m] = w
        part = lax.dot_general(
            w, I[j, pl.ds(frow, F), :], (((1,), (1,)), ((), ())), preferred_element_type=jnp.float32
        )
        G[m] = G[m] + part.reshape(HZ, nx, R, F)

    def loop_m(j, lo, hi):
        if j < NCH:
            lax.fori_loop(lo, hi, lambda m, c: (task(m, j), c)[1], 0)

    def loop_j(m, lo, hi):
        if lo < min(hi, NCH):
            lax.fori_loop(lo, min(hi, NCH), lambda j, c: (task(m, j), c)[1], 0)

    def slot(h, kz, kx):
        i = zi(kz)
        return T.at[2 * h + i // HZ, i % HZ, xi(kx)]

    for c in y_copies:
        c.wait_recv()
    for h in range(2):
        T[2 * h, 0, 0] = jnp.concatenate([Y[2 * h, :, 0:F], Y[2 * h + 1, :, 0:F]], axis=1)

    az, bz, bx, ax = {}, {}, {}, {}

    def z_send(store, h, kx, s):
        if s < lfz:
            store[kx, 1, s] = copy_to(slot(h, -s, kx), slot(h, -s - 1, kx), zf)
        if s < lbz:
            store[kx, -1, s] = copy_to(slot(h, s, kx), slot(h, s + 1, kx), zb)

    def z_wait(store, kx, s):
        for d in (1, -1):
            if (kx, d, s) in store:
                store[kx, d, s].wait_recv()

    def bx_send(kz):
        if kz in bx or kz not in ZO:
            return
        bx[kz] = [copy_to(slot(1, kz, 0), slot(1, kz, -1), xd(1))]
        if lbx:
            bx[kz].append(copy_to(slot(1, kz, 0), slot(1, kz, 1), xd(-1)))

    bx2 = {}

    def bx_fwd(kz):
        if kz in bx2 or kz not in ZO or lfx < 2:
            return
        bx[kz][0].wait_recv()
        bx2[kz] = copy_to(slot(1, kz, -1), slot(1, kz, -2), xd(1))

    def bx_fin(kz):
        if lfx < 2:
            bx[kz][0].wait_recv()
        else:
            bx2[kz].wait_recv()
        for c in bx[kz][1:]:
            c.wait_recv()

    z_send(bz, 1, 0, 0)
    for k in x_steps:
        ax[k] = copy_to(slot(0, 0, 0), slot(0, 0, -k), xd(k))
    z_send(az, 0, 0, 0)
    bx_send(0)
    others = [norm(-k, nx) for k in x_steps]
    for s in range(lfz):
        z_wait(bz, 0, s)
        z_send(bz, 1, 0, s + 1)
        bx_send(-s - 1)
        if s + 1 <= lbz:
            bx_send(s + 1)
        if s == 0:
            for k in x_steps[:2]:
                ax[k].wait_recv()
                z_send(az, 0, norm(-k, nx), 0)
            z_wait(az, 0, 0)
            z_send(az, 0, 0, 1)
            for k in x_steps[2:]:
                ax[k].wait_recv()
                z_send(az, 0, norm(-k, nx), 0)
            bx_fwd(0)
            forward_images(0)
        else:
            if s == 3:
                task(0, 0)
            for kx in others[:2]:
                z_wait(az, kx, s - 1)
                z_send(az, 0, kx, s)
            z_wait(az, 0, s)
            z_send(az, 0, 0, s + 1)
            bx_fwd(-s)
            bx_fwd(s)
            for kx in others[2:]:
                z_wait(az, kx, s - 1)
                z_send(az, 0, kx, s)
            if s == 2:
                forward_images(1)
                images_ready(0)
    if lfz < 3:
        forward_images(1)
        images_ready(0)
    if lfz < 4:
        task(0, 0)
    bx_fwd(-lfz)
    images_ready(1)
    loop_j(0, 1, 2)
    for kz in ZO[:HZ]:
        bx_fin(kz)
    loop_j(2, 0, 2)
    for kx in others:
        z_wait(az, kx, lfz - 1)
    loop_j(1, 0, 2)
    for kz in ZO[HZ:]:
        bx_fin(kz)
    forward_images(2)
    loop_j(3, 0, 2)
    images_ready(2)
    loop_m(2, 0, 4)
    forward_images(3)
    images_ready(3)

    NSUB = 2
    XS = nx // NSUB

    def azr_send(s):
        for sub in range(NSUB):
            xs = slice(sub * XS, (sub + 1) * XS)
            for d, length, sbuf, rbuf, dev in ((1, lfz, sAzf, rAzf, zf), (-1, lbz, sAzb, rAzb, zb)):
                if s >= length:
                    continue
                if s > 0:
                    azr[d, sub, s - 1].wait_recv()
                i = zi(d * (length - s))
                val = G[i // HZ, i % HZ, xs]
                if s > 0:
                    val = val + rbuf[s - 1, sub].astype(jnp.float32)
                sbuf[s, sub] = val.astype(sbuf.dtype)
                azr[d, sub, s] = copy_to(sbuf.at[s, sub], rbuf.at[s, sub], dev)

    azr = {}
    bxr = {}

    def bxr_send(s):
        for sub in range(2):
            for d, length, sbuf, rbuf in ((1, lfx, sBxf, rBxf), (-1, lbx, sBxb, rBxb)):
                if s >= length:
                    continue
                if s > 0:
                    bxr[d, sub, s - 1].wait_recv()
                val = G[2 + sub, :, xi(d * (length - s))]
                if s > 0:
                    val = val + rbuf[s - 1, sub].astype(jnp.float32)
                sbuf[s, sub] = val.astype(sbuf.dtype)
                bxr[d, sub, s] = copy_to(sbuf.at[s, sub], rbuf.at[s, sub], xd(d))

    LO = F // 128 * 128
    TW = 2 * F - LO

    def transpose_tile(m, c):
        rows = T[m].reshape(TM, 2 * F)
        own = jnp.where(feat == 0, rows[:, 0:TW], rows[:, LO : LO + TW])
        TT[m] = own.T
        return c

    def gi_step(j, c):
        off = pl.multiple_of(feat * (F - LO), 16)
        total = None
        for m in range(4):
            part = jnp.dot(TT[m, pl.ds(off, F), :], W[j, m], preferred_element_type=jnp.float32)
            total = part if total is None else total + part
        gI[j] = total
        return c

    gi_copies = []

    def gi_send(j):
        src = gI.at[j, :, pl.ds(pl.multiple_of((1 - core) * CH, 128), CH)]
        gi_copies.append(copy_to(src, gIr.at[j], sibling))

    out_copies = []

    def gi_finish(j):
        gi_copies[j].wait_recv()
        gIr[j] = gIr[j] + gI[j, :, pl.ds(ccol, CH)]
        c = pltpu.make_async_copy(gIr.at[j], gi_out.at[:, pl.ds(j * CH, CH)], loc.at[NCH + j])
        c.start()
        out_copies.append(c)

    last = NCH - 1
    early = lbz > 0 and zi(-lbz) // HZ == 1
    loop_m(last, 1, 2)
    if early:
        azr_send(0)
    loop_m(last, 2, 4)
    bxr_send(0)
    loop_m(last, 0, 1)
    if not early:
        azr_send(0)
    lax.fori_loop(0, 4, transpose_tile, 0)
    azr_send(1)
    gi_step(0, 0)
    gi_send(0)
    bxr_send(1)
    azr_send(2)
    if NCH > 1:
        gi_step(1, 0)
        gi_send(1)
    for sub in range(2):
        total = G[2 + sub, :, 0]
        for d, length, rbuf in ((1, lfx, rBxf), (-1, lbx, rBxb)):
            if length:
                bxr[d, sub, length - 1].wait_recv()
                total = total + rbuf[length - 1, sub].astype(jnp.float32)
        SB[sub] = total
    bzr = {}

    def bzr_send(s):
        for d, length, rbuf, dev in ((1, lfz, rBzf, zf), (-1, lbz, rBzb, zb)):
            if s >= length:
                continue
            i = zi(d * (length - s))
            src = SB.at[i // HZ, i % HZ]
            if s > 0:
                bzr[d, s - 1].wait_recv()
                rbuf[s - 1] = rbuf[s - 1] + src[...]
                src = rbuf.at[s - 1]
            bzr[d, s] = copy_to(src, rbuf.at[s], dev)

    bzr_send(0)
    azr_send(3)
    if NCH > 2:
        gi_step(2, 0)
        gi_send(2)
    bzr_send(1)
    for sub in range(NSUB):
        xs = slice(sub * XS, (sub + 1) * XS)
        total = G[0, 0, xs]
        for d, length, rbuf in ((1, lfz, rAzf), (-1, lbz, rAzb)):
            if length:
                azr[d, sub, length - 1].wait_recv()
                total = total + rbuf[length - 1, sub].astype(jnp.float32)
        SA[xs] = total
    axr = [copy_to(SA.at[xi(k)], rAx.at[n], xd(k)) for n, k in enumerate(x_steps)]
    if NCH > 3:
        gi_step(3, 0)
        gi_send(3)
    bzr_send(2)
    gi_finish(0)
    bzr_send(3)
    for j in range(1, NCH):
        gi_finish(j)
    endA = SA[0]
    for n, c in enumerate(axr):
        c.wait_recv()
        endA = endA + rAx[n]
    endB = SB[0, 0]
    for d, length, rbuf in ((1, lfz, rBzf), (-1, lbz, rBzb)):
        if length:
            bzr[d, length - 1].wait_recv()
            endB = endB + rbuf[length - 1]
    first = yh == 0
    finY[...] = jnp.where(first, endB, endA)
    last_copy = copy_to(finY, rY, dev_y)
    own = jnp.where(first, endA, endB)
    last_copy.wait_recv()
    gt_out[...] = own + rY[...]

    for c in started:
        c.wait_send()
    for c in out_copies:
        c.wait()


def build(nz, ny, nx, F, C, total_images):
    lfx, lbx = chain_lengths(nx)
    lfz, lbz = chain_lengths(nz)
    hz, xs = nz // 2, nx // 2
    tm = hz * nx * R
    nch = C // CH
    tw = 2 * F - F // 128 * 128
    f32, bf16 = jnp.float32, jnp.bfloat16

    def chain(n, shape, dtype):
        return pltpu.VMEM((max(n, 1),) + shape, dtype)

    scratch = [
        pltpu.VMEM((4, hz, nx, R, 2 * F), bf16),
        pltpu.VMEM((4, tw, tm), bf16),
        pltpu.VMEM((nch, 2 * F, 2 * CH), bf16),
        pltpu.VMEM((nch, 4, tm, 2 * CH), bf16),
        pltpu.VMEM((4, hz, nx, R, F), f32),
        pltpu.VMEM((nch, F, 2 * CH), f32),
        pltpu.VMEM((nch, F, CH), f32),
        pltpu.VMEM((4, tm, 128), jnp.int32),
        pltpu.VMEM((4, R, -(-F // 128) * 128), bf16),
        *[chain(n, (2, xs, R, F), WIRE_A) for n in (lfz, lbz, lfz, lbz)],
        *[chain(n, (2, hz, R, F), WIRE_B) for n in (lfx, lbx, lfx, lbx)],
        pltpu.VMEM((nx, R, F), f32),
        pltpu.VMEM((3, R, F), f32),
        pltpu.VMEM((2, hz, R, F), f32),
        chain(lfz, (R, F), f32),
        chain(lbz, (R, F), f32),
        pltpu.VMEM((R, F), f32),
        pltpu.VMEM((R, F), f32),
        pltpu.SemaphoreType.DMA((140,)),
        pltpu.SemaphoreType.DMA((140,)),
        pltpu.SemaphoreType.DMA((2 * nch,)),
    ]
    smem = pl.BlockSpec(memory_space=pltpu.SMEM)
    vmem = pl.BlockSpec(memory_space=pltpu.VMEM)
    hbm = pl.BlockSpec(memory_space=pl.ANY)

    def body(images, texts, img_group, txt_group, temp, bias, loss_scale):
        gi, gt = pl.pallas_call(
            functools.partial(kernel, (nz, ny, nx, F, C, total_images)),
            out_shape=(jax.ShapeDtypeStruct((F, C), f32), jax.ShapeDtypeStruct((R, F), f32)),
            in_specs=[hbm, vmem, smem, smem, smem, smem, smem],
            out_specs=(hbm, vmem),
            scratch_shapes=scratch,
            compiler_params=pltpu.CompilerParams(
                collective_id=0, has_side_effects=True, vmem_limit_bytes=56 * 1024 * 1024
            ),
        )(images.T, texts, img_group, txt_group, temp.reshape(1), bias.reshape(1), loss_scale.reshape(1))
        return gi.T, gt

    return body


def solution(mesh):
    body = build(NZ, NY, NX, 576, 1024, 131072)
    in_specs = (P("blk", "feat"), P("blk", "feat"), P(), P(), P(), P(), P())
    out_specs = (P("blk", "feat"), P("blk", "feat"))
    return jax.shard_map(body, mesh=mesh, in_specs=in_specs, out_specs=out_specs, check_vma=False)
```

```python
import functools

import jax
import jax.numpy as jnp
from jax import lax
from jax.experimental import pallas as pl
from jax.experimental.pallas import tpu as pltpu
from jax.sharding import PartitionSpec as P

MESH = pl.DeviceIdType.MESH
NZ, NY, NX = 8, 2, 4
R = 16
CH = 256
WIRE_A = jnp.float32
WIRE_B = jnp.bfloat16


def chain_lengths(n):
    return n // 2, (n - 1) // 2


def near_first(n):
    lf, lb = chain_lengths(n)
    return sorted(range(-lf, lb + 1), key=lambda k: (abs(k), k))


def kernel(
    cfg,
    img_ref, txt_hbm, ig_hbm, tg_hbm, temp_hbm, bias_hbm, scale_hbm,
    gi_out, gt_out,
    txt_ref, ig_ref, tg_ref, temp_ref, bias_ref, scale_ref,
    T, TT, I, W, G, gI, gIr, tgv, Y,
    sAzf, sAzb, rAzf, rAzb, sBxf, sBxb, rBxf, rBxb,
    SA, rAx, SB, rBz, finY, rY,
    send, recv, loc,
):
    nz, ny, nx, F, C, total_images = cfg
    NCH = C // CH
    HZ = nz // 2
    TM = HZ * nx * R
    W2 = 2 * CH
    ZO, XO = near_first(nz), near_first(nx)
    lfz, lbz = chain_lengths(nz)
    lfx, lbx = chain_lengths(nx)

    def norm(k, n):
        return k - n if k > (n - 1) // 2 else k

    def zi(k):
        return ZO.index(norm(k, nz))

    def xi(k):
        return XO.index(norm(k, nx))

    blk = lax.axis_index("blk")
    feat = lax.axis_index("feat")
    core = lax.rem(blk, 2)
    x = lax.rem(blk // 2, nx)
    yh = lax.rem(blk // (2 * nx), ny)
    z = blk // (2 * nx * ny)
    step_dir = 1 - 2 * core

    def at(z_, yh_, x_, core_, feat_):
        return (((z_ * ny + yh_) * nx + x_) * 2 + core_, feat_)

    def zz(k):
        return lax.rem(z + step_dir * k + 2 * nz, nz)

    def xx(k):
        return lax.rem(x + step_dir * k + 2 * nx, nx)

    sibling = at(z, yh, x, 1 - core, feat)
    dev_f = at(z, yh, x, core, 1 - feat)
    dev_y = at(z, 1 - yh, x, core, feat)
    dev_d = at(z, 1 - yh, x, core, 1 - feat)
    zf, zb = at(zz(1), yh, x, core, feat), at(zz(-1), yh, x, core, feat)

    def xd(k):
        return at(z, yh, xx(k), core, feat)

    def zd(k):
        return at(zz(k), yh, x, core, feat)

    x_steps = [k for k in (1, -1, 2) if k < nx and (k != -1 or nx > 2)]
    txt_copy = pltpu.make_async_copy(txt_hbm, txt_ref, loc.at[NCH])
    txt_copy.start()
    small = [
        pltpu.make_async_copy(src, dst, loc.at[NCH + 1 + n])
        for n, (src, dst) in enumerate(
            ((ig_hbm, ig_ref), (tg_hbm, tg_ref), (temp_hbm, temp_ref), (bias_hbm, bias_ref), (scale_hbm, scale_ref))
        )
    ]
    for c in small:
        c.start()
    barrier = pltpu.get_barrier_semaphore()
    partners = [sibling, dev_f, dev_y, dev_d, zf, zb, zd(2), zd(-2)] + [xd(k) for k in x_steps]
    for dev in partners:
        pl.semaphore_signal(barrier, inc=1, device_id=dev, device_id_type=MESH)

    ccol = pl.multiple_of(core * CH, 128)
    frow = pl.multiple_of(feat * F, 16)
    orow = pl.multiple_of((1 - feat) * F, 16)

    def img_src(j):
        return img_ref.at[:, pl.ds(j * CH, CH)]

    def img_dst(j):
        return I.at[j, pl.ds(frow, F), pl.ds(ccol, CH)]

    own_copies = [pltpu.make_async_copy(img_src(j), img_dst(j), loc.at[j]) for j in range(NCH)]
    for c in own_copies:
        c.start()
    me = yh * 2 + feat
    txt_copy.wait()
    Y[me, :, 0:F] = txt_ref[...]
    for c in small:
        c.wait()
    for i, kz in enumerate(ZO):
        t, a = divmod(i, HZ)
        for h in range(2):
            group = jnp.full((nx * R, 128), tg_ref[zz(kz) * ny + h], jnp.int32)
            tgv[2 * h + t, a * nx * R : (a + 1) * nx * R, :] = group
    G[...] = jnp.zeros_like(G)

    pl.semaphore_wait(barrier, len(partners))

    count = [0]
    started = []

    def copy_to(src, dst, dev):
        i = count[0]
        count[0] += 1
        c = pltpu.make_async_remote_copy(
            src_ref=src, dst_ref=dst, send_sem=send.at[i], recv_sem=recv.at[i], device_id=dev, device_id_type=MESH
        )
        c.start()
        started.append(c)
        return c

    y_copies = [copy_to(Y.at[me], Y.at[me], dev) for dev in (dev_f, dev_y, dev_d)]
    img_copies = [copy_to(img_src(j), img_dst(j), dev_f) for j in range(NCH)]
    sib_copies = [copy_to(img_src(j), img_dst(j), sibling) for j in range(NCH)]
    fwd_copies = {}

    def forward_images(j):
        if j < NCH:
            img_copies[j].wait_recv()
            ref = I.at[j, pl.ds(orow, F), pl.ds(ccol, CH)]
            fwd_copies[j] = copy_to(ref, ref, sibling)

    ready = set()

    def images_ready(j):
        if j < NCH and j not in ready:
            ready.add(j)
            own_copies[j].wait()
            sib_copies[j].wait_recv()
            fwd_copies[j].wait_recv()

    temp, bias = temp_ref[0], bias_ref[0]
    factor = -(scale_ref[0] * temp / total_images)

    def task(m, j):
        raw = jnp.dot(T[m].reshape(TM, 2 * F), I[j], preferred_element_type=jnp.float32)
        tg = tgv[m]
        parts = []
        for q in range(W2 // 128):
            per = CH // 128
            group = ig_ref[(blk - core + q // per) * (C // 128) + j * per + q % per]
            logit = temp * raw[:, q * 128 : (q + 1) * 128] + bias
            same = tg == group
            p = 1.0 / (1.0 + jnp.exp(jnp.where(same, logit, -logit)))
            parts.append((jnp.where(same, factor, -factor) * p).astype(jnp.bfloat16))
        w = jnp.concatenate(parts, axis=1)
        W[j, m] = w
        part = lax.dot_general(
            w, I[j, pl.ds(frow, F), :], (((1,), (1,)), ((), ())), preferred_element_type=jnp.float32
        )
        G[m] = G[m] + part.reshape(HZ, nx, R, F)

    def loop_m(j, lo, hi):
        if j < NCH:
            lax.fori_loop(lo, hi, lambda m, c: (task(m, j), c)[1], 0)

    def loop_j(m, lo, hi):
        if lo < min(hi, NCH):
            lax.fori_loop(lo, min(hi, NCH), lambda j, c: (task(m, j), c)[1], 0)

    def slot(h, kz, kx):
        i = zi(kz)
        return T.at[2 * h + i // HZ, i % HZ, xi(kx)]

    for c in y_copies:
        c.wait_recv()
    for h in range(2):
        T[2 * h, 0, 0] = jnp.concatenate([Y[2 * h, :, 0:F], Y[2 * h + 1, :, 0:F]], axis=1)

    az, bz, bx, ax = {}, {}, {}, {}

    def z_send(store, h, kx, s):
        if s < lfz:
            store[kx, 1, s] = copy_to(slot(h, -s, kx), slot(h, -s - 1, kx), zf)
        if s < lbz:
            store[kx, -1, s] = copy_to(slot(h, s, kx), slot(h, s + 1, kx), zb)

    def z_wait(store, kx, s):
        for d in (1, -1):
            if (kx, d, s) in store:
                store[kx, d, s].wait_recv()

    def bx_send(kz):
        if kz in bx or kz not in ZO:
            return
        bx[kz] = [copy_to(slot(1, kz, 0), slot(1, kz, -1), xd(1))]
        if lbx:
            bx[kz].append(copy_to(slot(1, kz, 0), slot(1, kz, 1), xd(-1)))

    bx2 = {}

    def bx_fwd(kz):
        if kz in bx2 or kz not in ZO or lfx < 2:
            return
        bx[kz][0].wait_recv()
        bx2[kz] = copy_to(slot(1, kz, -1), slot(1, kz, -2), xd(1))

    def bx_fin(kz):
        if lfx < 2:
            bx[kz][0].wait_recv()
        else:
            bx2[kz].wait_recv()
        for c in bx[kz][1:]:
            c.wait_recv()

    def bz_send(k, frm=0):
        bz[k] = copy_to(slot(1, frm, 0), slot(1, frm - (k - SIGN[k] * abs(frm)), 0), zd(k - SIGN[k] * abs(frm)))

    SIGN = {1: 1, 2: 1, 3: 1, 4: 1, -1: -1, -2: -1, -3: -1}
    for k in (1, -1, 2, -2):
        bz_send(k)
    for k in x_steps:
        ax[k] = copy_to(slot(0, 0, 0), slot(0, 0, -k), xd(k))
    z_send(az, 0, 0, 0)
    bx_send(0)
    others = [norm(-k, nx) for k in x_steps]

    def az_on(kxs, s):
        for kx in kxs:
            z_wait(az, kx, s - 1)
            z_send(az, 0, kx, s)

    def bz_got(*ks):
        for k in ks:
            bz[k].wait_recv()
        for k in ks:
            bx_send(-k)

    bz_got(1, -1)
    for k in x_steps[:2]:
        ax[k].wait_recv()
        z_send(az, 0, norm(-k, nx), 0)
    bz[2].wait_recv()
    bz_send(4, -2)
    bz_send(3, -2)
    bz[-2].wait_recv()
    bz_send(-3, 2)
    az_on([0], 1)
    bx_send(-2)
    bx_send(2)
    for k in x_steps[2:]:
        ax[k].wait_recv()
        z_send(az, 0, norm(-k, nx), 0)
    bx_fwd(0)
    az_on(others[:2], 1)
    bx_fwd(-1)
    bx_fwd(1)
    az_on([0], 2)
    az_on(others[2:], 1)
    bz_got(3, -3, 4)
    bx_fwd(-2)
    forward_images(0)
    az_on(others[:2], 2)
    az_on([0], 3)
    az_on(others[2:], 2)
    for kz in ZO[:HZ]:
        bx_fin(kz)
    images_ready(0)
    task(2, 0)
    bx_fwd(2)
    bx_fwd(-3)
    bx_fwd(3)
    bx_fwd(-4)
    az_on(others[:2], 3)
    az_on(others[2:], 3)
    task(0, 0)
    forward_images(1)
    for kz in ZO[HZ:]:
        bx_fin(kz)
    task(3, 0)
    images_ready(1)
    lax.fori_loop(0, 3, lambda i, c: (task(i + (i > 0), 1), c)[1], 0)
    for kx in [0] + others:
        z_wait(az, kx, lfz - 1)
    forward_images(2)
    loop_j(1, 0, 2)
    images_ready(2)
    loop_m(2, 0, 4)
    forward_images(3)
    images_ready(3)

    NSUB = 2
    XS = nx // NSUB

    def azr_send(s):
        for sub in range(NSUB):
            xs = slice(sub * XS, (sub + 1) * XS)
            for d, length, sbuf, rbuf, dev in ((1, lfz, sAzf, rAzf, zf), (-1, lbz, sAzb, rAzb, zb)):
                if s >= length:
                    continue
                if s > 0:
                    azr[d, sub, s - 1].wait_recv()
                i = zi(d * (length - s))
                val = G[i // HZ, i % HZ, xs]
                if s > 0:
                    val = val + rbuf[s - 1, sub].astype(jnp.float32)
                sbuf[s, sub] = val.astype(sbuf.dtype)
                azr[d, sub, s] = copy_to(sbuf.at[s, sub], rbuf.at[s, sub], dev)

    azr = {}
    bxr = {}

    def bxr_send(s):
        for sub in range(2):
            for d, length, sbuf, rbuf in ((1, lfx, sBxf, rBxf), (-1, lbx, sBxb, rBxb)):
                if s >= length:
                    continue
                if s > 0:
                    bxr[d, sub, s - 1].wait_recv()
                val = G[2 + sub, :, xi(d * (length - s))]
                if s > 0:
                    val = val + rbuf[s - 1, sub].astype(jnp.float32)
                sbuf[s, sub] = val.astype(sbuf.dtype)
                bxr[d, sub, s] = copy_to(sbuf.at[s, sub], rbuf.at[s, sub], xd(d))

    LO = F // 128 * 128
    TW = 2 * F - LO

    def transpose_tile(m, c):
        rows = T[m].reshape(TM, 2 * F)
        own = jnp.where(feat == 0, rows[:, 0:TW], rows[:, LO : LO + TW])
        TT[m] = own.T
        return c

    def gi_step(j, c):
        off = pl.multiple_of(feat * (F - LO), 16)
        total = None
        for m in range(4):
            part = jnp.dot(TT[m, pl.ds(off, F), :], W[j, m], preferred_element_type=jnp.float32)
            total = part if total is None else total + part
        gI[j] = total
        return c

    gi_copies = []

    def gi_send(j):
        src = gI.at[j, :, pl.ds(pl.multiple_of((1 - core) * CH, 128), CH)]
        gi_copies.append(copy_to(src, gIr.at[j], sibling))

    def gi_finish(j):
        gi_copies[j].wait_recv()
        gi_out[:, j * CH : (j + 1) * CH] = gIr[j] + gI[j, :, pl.ds(ccol, CH)]

    last = NCH - 1
    early = lbz > 0 and zi(-lbz) // HZ == 1
    loop_m(last, 1, 2)
    if early:
        azr_send(0)
    loop_m(last, 2, 4)
    bxr_send(0)
    loop_m(last, 0, 1)
    if not early:
        azr_send(0)
    lax.fori_loop(0, 4, transpose_tile, 0)
    azr_send(1)
    gi_step(0, 0)
    gi_send(0)
    bxr_send(1)
    azr_send(2)
    if NCH > 1:
        gi_step(1, 0)
        gi_send(1)
    for sub in range(2):
        total = G[2 + sub, :, 0]
        for d, length, rbuf in ((1, lfx, rBxf), (-1, lbx, rBxb)):
            if length:
                bxr[d, sub, length - 1].wait_recv()
                total = total + rbuf[length - 1, sub].astype(jnp.float32)
        SB[sub] = total
    bzr = {}

    def bzr_first():
        for n, k, hop in ((0, 4, 2), (1, 3, 2), (2, -3, -2), (3, -2, -2)):
            i = zi(k)
            bzr[n] = copy_to(SB.at[i // HZ, i % HZ], rBz.at[n], zd(hop))

    def bzr_second():
        for n, k in ((0, 2), (1, 1), (2, -1)):
            i = zi(k)
            bzr[n].wait_recv()
            rBz[n] = rBz[n] + SB[i // HZ, i % HZ]
            bzr[4 + n] = copy_to(rBz.at[n], rBz.at[4 + n], zd(k))

    bzr_first()
    azr_send(3)
    if NCH > 2:
        gi_step(2, 0)
        gi_send(2)
    bzr_second()
    for sub in range(NSUB):
        xs = slice(sub * XS, (sub + 1) * XS)
        total = G[0, 0, xs]
        for d, length, rbuf in ((1, lfz, rAzf), (-1, lbz, rAzb)):
            if length:
                azr[d, sub, length - 1].wait_recv()
                total = total + rbuf[length - 1, sub].astype(jnp.float32)
        SA[xs] = total
    axr = [copy_to(SA.at[xi(k)], rAx.at[n], xd(k)) for n, k in enumerate(x_steps)]
    if NCH > 3:
        gi_step(3, 0)
        gi_send(3)
    for j in range(NCH):
        gi_finish(j)
    endA = SA[0]
    for n, c in enumerate(axr):
        c.wait_recv()
        endA = endA + rAx[n]
    endB = SB[0, 0]
    for n in range(3, 7):
        bzr[n].wait_recv()
        endB = endB + rBz[n]
    first = yh == 0
    finY[...] = jnp.where(first, endB, endA)
    last_copy = copy_to(finY, rY, dev_y)
    own = jnp.where(first, endA, endB)
    last_copy.wait_recv()
    gt_out[...] = own + rY[...]

    for c in started:
        c.wait_send()


def build(nz, ny, nx, F, C, total_images):
    lfx, lbx = chain_lengths(nx)
    lfz, lbz = chain_lengths(nz)
    hz, xs = nz // 2, nx // 2
    tm = hz * nx * R
    nch = C // CH
    tw = 2 * F - F // 128 * 128
    f32, bf16 = jnp.float32, jnp.bfloat16

    def chain(n, shape, dtype):
        return pltpu.VMEM((max(n, 1),) + shape, dtype)

    smem = pltpu.SMEM
    scratch = [
        pltpu.VMEM((R, F), bf16),
        smem((C * nz * ny * nx * 2 // 128,), jnp.int32),
        smem((nz * ny,), jnp.int32),
        smem((1,), f32),
        smem((1,), f32),
        smem((1,), f32),
        pltpu.VMEM((4, hz, nx, R, 2 * F), bf16),
        pltpu.VMEM((4, tw, tm), bf16),
        pltpu.VMEM((nch, 2 * F, 2 * CH), bf16),
        pltpu.VMEM((nch, 4, tm, 2 * CH), bf16),
        pltpu.VMEM((4, hz, nx, R, F), f32),
        pltpu.VMEM((nch, F, 2 * CH), f32),
        pltpu.VMEM((nch, F, CH), f32),
        pltpu.VMEM((4, tm, 128), jnp.int32),
        pltpu.VMEM((4, R, -(-F // 128) * 128), bf16),
        *[chain(n, (2, xs, R, F), WIRE_A) for n in (lfz, lbz, lfz, lbz)],
        *[chain(n, (2, hz, R, F), WIRE_B) for n in (lfx, lbx, lfx, lbx)],
        pltpu.VMEM((nx, R, F), f32),
        pltpu.VMEM((3, R, F), f32),
        pltpu.VMEM((2, hz, R, F), f32),
        pltpu.VMEM((7, R, F), f32),
        pltpu.VMEM((R, F), f32),
        pltpu.VMEM((R, F), f32),
        pltpu.SemaphoreType.DMA((140,)),
        pltpu.SemaphoreType.DMA((140,)),
        pltpu.SemaphoreType.DMA((nch + 6,)),
    ]
    vmem = pl.BlockSpec(memory_space=pltpu.VMEM)
    hbm = pl.BlockSpec(memory_space=pl.ANY)

    def body(images, texts, img_group, txt_group, temp, bias, loss_scale):
        gi, gt = pl.pallas_call(
            functools.partial(kernel, (nz, ny, nx, F, C, total_images)),
            out_shape=(pltpu.VMEM((F, C), f32), pltpu.VMEM((R, F), f32)),
            in_specs=[hbm] * 7,
            out_specs=(vmem, vmem),
            scratch_shapes=scratch,
            compiler_params=pltpu.CompilerParams(
                collective_id=0, has_side_effects=True, vmem_limit_bytes=56 * 1024 * 1024
            ),
        )(images.T, texts, img_group, txt_group, temp.reshape(1), bias.reshape(1), loss_scale.reshape(1))
        return gi.T, gt

    return body


def solution(mesh):
    body = build(NZ, NY, NX, 576, 1024, 131072)
    in_specs = (P("blk", "feat"), P("blk", "feat"), P(), P(), P(), P(), P())
    out_specs = (P("blk", "feat"), P("blk", "feat"))
    return jax.shard_map(body, mesh=mesh, in_specs=in_specs, out_specs=out_specs, check_vma=False)
```

```python
import functools

import jax
import jax.numpy as jnp
from jax import lax
from jax.experimental import pallas as pl
from jax.experimental.pallas import tpu as pltpu
from jax.sharding import PartitionSpec as P

MESH = pl.DeviceIdType.MESH
NZ, NY, NX = 8, 2, 4
R = 16
CH = 256
WIRE_A = jnp.bfloat16
WIRE_B = jnp.bfloat16


def chain_lengths(n):
    return n // 2, (n - 1) // 2


def near_first(n):
    lf, lb = chain_lengths(n)
    return sorted(range(-lf, lb + 1), key=lambda k: (abs(k), k))


def kernel(
    cfg,
    img_ref, txt_hbm, ig_hbm, tg_hbm, temp_hbm, bias_hbm, scale_hbm,
    gi_out, gt_out,
    txt_ref, ig_ref, tg_ref, temp_ref, bias_ref, scale_ref,
    T, TT, I, W, G, gI, gIr, tgv, Y,
    sAzf, sAzb, rAzf, rAzb, sBxf, sBxb, rBxf, rBxb,
    SA, rAx, SB, rBz, finY, rY,
    send, recv, loc,
):
    nz, ny, nx, F, C, total_images = cfg
    NCH = C // CH
    HZ = nz // 2
    TM = HZ * nx * R
    W2 = 2 * CH
    ZO, XO = near_first(nz), near_first(nx)
    lfz, lbz = chain_lengths(nz)
    lfx, lbx = chain_lengths(nx)

    def norm(k, n):
        return k - n if k > (n - 1) // 2 else k

    def zi(k):
        return ZO.index(norm(k, nz))

    def xi(k):
        return XO.index(norm(k, nx))

    blk = lax.axis_index("blk")
    feat = lax.axis_index("feat")
    core = lax.rem(blk, 2)
    x = lax.rem(blk // 2, nx)
    yh = lax.rem(blk // (2 * nx), ny)
    z = blk // (2 * nx * ny)
    step_dir = 1 - 2 * core

    def at(z_, yh_, x_, core_, feat_):
        return (((z_ * ny + yh_) * nx + x_) * 2 + core_, feat_)

    def zz(k):
        return lax.rem(z + step_dir * k + 2 * nz, nz)

    def xx(k):
        return lax.rem(x + step_dir * k + 2 * nx, nx)

    sibling = at(z, yh, x, 1 - core, feat)
    dev_f = at(z, yh, x, core, 1 - feat)
    dev_y = at(z, 1 - yh, x, core, feat)
    dev_d = at(z, 1 - yh, x, core, 1 - feat)
    zf, zb = at(zz(1), yh, x, core, feat), at(zz(-1), yh, x, core, feat)

    def xd(k):
        return at(z, yh, xx(k), core, feat)

    def zd(k):
        return at(zz(k), yh, x, core, feat)

    x_steps = [k for k in (1, -1, 2) if k < nx and (k != -1 or nx > 2)]
    txt_copy = pltpu.make_async_copy(txt_hbm, txt_ref, loc.at[NCH])
    txt_copy.start()
    small = [
        pltpu.make_async_copy(src, dst, loc.at[NCH + 1 + n])
        for n, (src, dst) in enumerate(
            ((ig_hbm, ig_ref), (tg_hbm, tg_ref), (temp_hbm, temp_ref), (bias_hbm, bias_ref), (scale_hbm, scale_ref))
        )
    ]
    for c in small:
        c.start()
    barrier = pltpu.get_barrier_semaphore()
    partners = [sibling, dev_f, dev_y, dev_d, zf, zb, zd(2), zd(-2)] + [xd(k) for k in x_steps]
    for dev in partners:
        pl.semaphore_signal(barrier, inc=1, device_id=dev, device_id_type=MESH)

    ccol = pl.multiple_of(core * CH, 128)
    frow = pl.multiple_of(feat * F, 16)
    orow = pl.multiple_of((1 - feat) * F, 16)

    def img_src(j):
        return img_ref.at[:, pl.ds(j * CH, CH)]

    def img_dst(j):
        return I.at[j, pl.ds(frow, F), pl.ds(ccol, CH)]

    own_copies = [pltpu.make_async_copy(img_src(j), img_dst(j), loc.at[j]) for j in range(NCH)]
    for c in own_copies:
        c.start()
    me = yh * 2 + feat
    txt_copy.wait()
    Y[me, :, 0:F] = txt_ref[...]
    for c in small:
        c.wait()
    for i, kz in enumerate(ZO):
        t, a = divmod(i, HZ)
        for h in range(2):
            group = jnp.full((nx * R, 128), tg_ref[zz(kz) * ny + h], jnp.int32)
            tgv[2 * h + t, a * nx * R : (a + 1) * nx * R, :] = group
    G[...] = jnp.zeros_like(G)

    pl.semaphore_wait(barrier, len(partners))

    count = [0]
    started = []

    def copy_to(src, dst, dev):
        i = count[0]
        count[0] += 1
        c = pltpu.make_async_remote_copy(
            src_ref=src, dst_ref=dst, send_sem=send.at[i], recv_sem=recv.at[i], device_id=dev, device_id_type=MESH
        )
        c.start()
        started.append(c)
        return c

    y_copies = [copy_to(Y.at[me], Y.at[me], dev) for dev in (dev_f, dev_y, dev_d)]
    img_copies = [copy_to(img_src(j), img_dst(j), dev_f) for j in range(NCH)]
    sib_copies = [copy_to(img_src(j), img_dst(j), sibling) for j in range(NCH)]
    fwd_copies = {}

    def forward_images(j):
        if j < NCH:
            img_copies[j].wait_recv()
            ref = I.at[j, pl.ds(orow, F), pl.ds(ccol, CH)]
            fwd_copies[j] = copy_to(ref, ref, sibling)

    ready = set()

    def images_ready(j):
        if j < NCH and j not in ready:
            ready.add(j)
            own_copies[j].wait()
            sib_copies[j].wait_recv()
            fwd_copies[j].wait_recv()

    temp, bias = temp_ref[0], bias_ref[0]
    factor = -(scale_ref[0] * temp / total_images)

    def task(m, j, n=1):
        raw = jnp.dot(T[pl.ds(m, n)].reshape(n * TM, 2 * F), I[j], preferred_element_type=jnp.float32)
        tg = tgv[pl.ds(m, n)].reshape(n * TM, 128)
        parts = []
        for q in range(W2 // 128):
            per = CH // 128
            group = ig_ref[(blk - core + q // per) * (C // 128) + j * per + q % per]
            logit = temp * raw[:, q * 128 : (q + 1) * 128] + bias
            same = tg == group
            p = 1.0 / (1.0 + jnp.exp(jnp.where(same, logit, -logit)))
            parts.append((jnp.where(same, factor, -factor) * p).astype(jnp.bfloat16))
        w = jnp.concatenate(parts, axis=1)
        W[j, pl.ds(m, n)] = w.reshape(n, TM, W2)
        part = lax.dot_general(
            w, I[j, pl.ds(frow, F), :], (((1,), (1,)), ((), ())), preferred_element_type=jnp.float32
        )
        G[pl.ds(m, n)] = G[pl.ds(m, n)] + part.reshape(n, HZ, nx, R, F)

    def slot(h, kz, kx):
        i = zi(kz)
        return T.at[2 * h + i // HZ, i % HZ, xi(kx)]

    for c in y_copies:
        c.wait_recv()
    for h in range(2):
        T[2 * h, 0, 0] = jnp.concatenate([Y[2 * h, :, 0:F], Y[2 * h + 1, :, 0:F]], axis=1)

    az, bz, bx, ax = {}, {}, {}, {}

    def z_send(store, h, kx, s):
        if s < lfz:
            store[kx, 1, s] = copy_to(slot(h, -s, kx), slot(h, -s - 1, kx), zf)
        if s < lbz:
            store[kx, -1, s] = copy_to(slot(h, s, kx), slot(h, s + 1, kx), zb)

    def z_wait(store, kx, s):
        for d in (1, -1):
            if (kx, d, s) in store:
                store[kx, d, s].wait_recv()

    def bx_send(kz):
        if kz in bx or kz not in ZO:
            return
        bx[kz] = [copy_to(slot(1, kz, 0), slot(1, kz, -1), xd(1))]
        if lbx:
            bx[kz].append(copy_to(slot(1, kz, 0), slot(1, kz, 1), xd(-1)))

    bx2 = {}

    def bx_fwd(kz):
        if kz in bx2 or kz not in ZO or lfx < 2:
            return
        bx[kz][0].wait_recv()
        bx2[kz] = copy_to(slot(1, kz, -1), slot(1, kz, -2), xd(1))

    def bx_fin(kz):
        if lfx < 2:
            bx[kz][0].wait_recv()
        else:
            bx2[kz].wait_recv()
        for c in bx[kz][1:]:
            c.wait_recv()

    def bz_send(k, frm=0):
        bz[k] = copy_to(slot(1, frm, 0), slot(1, frm - (k - SIGN[k] * abs(frm)), 0), zd(k - SIGN[k] * abs(frm)))

    SIGN = {1: 1, 2: 1, 3: 1, 4: 1, -1: -1, -2: -1, -3: -1}
    for k in (1, -1, 2, -2):
        bz_send(k)
    for k in x_steps:
        ax[k] = copy_to(slot(0, 0, 0), slot(0, 0, -k), xd(k))
    z_send(az, 0, 0, 0)
    bx_send(0)
    others = [norm(-k, nx) for k in x_steps]

    def az_on(kxs, s):
        for kx in kxs:
            z_wait(az, kx, s - 1)
            z_send(az, 0, kx, s)

    def bz_got(*ks):
        for k in ks:
            bz[k].wait_recv()
        for k in ks:
            bx_send(-k)

    bz_got(1, -1)
    for k in x_steps[:2]:
        ax[k].wait_recv()
        z_send(az, 0, norm(-k, nx), 0)
    bz[2].wait_recv()
    bz_send(4, -2)
    bz_send(3, -2)
    bz[-2].wait_recv()
    bz_send(-3, 2)
    az_on([0], 1)
    bx_send(-2)
    bx_send(2)
    for k in x_steps[2:]:
        ax[k].wait_recv()
        z_send(az, 0, norm(-k, nx), 0)
    bx_fwd(0)
    az_on(others[:2], 1)
    bx_fwd(-1)
    bx_fwd(1)
    az_on([0], 2)
    az_on(others[2:], 1)
    bz_got(3, -3, 4)
    bx_fwd(-2)
    forward_images(0)
    az_on(others[:2], 2)
    az_on([0], 3)
    az_on(others[2:], 2)
    for kz in ZO[:HZ]:
        bx_fin(kz)
    images_ready(0)
    task(2, 0)
    bx_fwd(2)
    bx_fwd(-3)
    bx_fwd(3)
    bx_fwd(-4)
    az_on(others[:2], 3)
    az_on(others[2:], 3)
    task(0, 0)
    forward_images(1)
    for kz in ZO[HZ:]:
        bx_fin(kz)
    task(3, 0)
    images_ready(1)
    task(2, 1, 2)
    for kx in [0] + others:
        z_wait(az, kx, lfz - 1)
    forward_images(2)
    task(1, 0)
    task(0, 1, 2)
    images_ready(2)
    task(0, 2, 4)
    forward_images(3)
    images_ready(3)

    NSUB = 2
    XS = nx // NSUB

    def azr_send(s):
        for sub in range(NSUB):
            xs = slice(sub * XS, (sub + 1) * XS)

            def block(k):
                i = zi(k)
                return G[i // HZ, i % HZ, xs]

            def put(key, val, sbuf, rbuf, dev):
                sbuf[key[1], sub] = val.astype(sbuf.dtype)
                azr[key[0], sub, key[1]] = copy_to(sbuf.at[key[1], sub], rbuf.at[key[1], sub], dev)

            if s == 0:
                put((1, 0), block(4), sAzf, rAzf, zd(2))
                put((1, 1), block(3), sAzf, rAzf, zf)
            elif s == 1:
                azr[1, sub, 0].wait_recv()
                azr[1, sub, 1].wait_recv()
                val = block(2) + rAzf[0, sub].astype(jnp.float32) + rAzf[1, sub].astype(jnp.float32)
                put((1, 2), val, sAzf, rAzf, zf)
            else:
                azr[1, sub, 2].wait_recv()
                put((1, 3), block(1) + rAzf[2, sub].astype(jnp.float32), sAzf, rAzf, zf)
            val = block(s - 3)
            if s > 0:
                azr[-1, sub, s - 1].wait_recv()
                val = val + rAzb[s - 1, sub].astype(jnp.float32)
            put((-1, s), val, sAzb, rAzb, zb)

    azr = {}
    bxr = {}

    def bxr_send(s):
        for sub in range(2):
            for d, length, sbuf, rbuf in ((1, lfx, sBxf, rBxf), (-1, lbx, sBxb, rBxb)):
                if s >= length:
                    continue
                if s > 0:
                    bxr[d, sub, s - 1].wait_recv()
                val = G[2 + sub, :, xi(d * (length - s))]
                if s > 0:
                    val = val + rbuf[s - 1, sub].astype(jnp.float32)
                sbuf[s, sub] = val.astype(sbuf.dtype)
                bxr[d, sub, s] = copy_to(sbuf.at[s, sub], rbuf.at[s, sub], xd(d))

    LO = F // 128 * 128
    TW = 2 * F - LO

    def transpose_tile(m, c):
        rows = T[m].reshape(TM, 2 * F)
        own = jnp.where(feat == 0, rows[:, 0:TW], rows[:, LO : LO + TW])
        TT[m] = own.T
        return c

    def gi_step(j, c):
        off = pl.multiple_of(feat * (F - LO), 16)
        total = None
        for m in range(4):
            part = jnp.dot(TT[m, pl.ds(off, F), :], W[j, m], preferred_element_type=jnp.float32)
            total = part if total is None else total + part
        gI[j] = total
        return c

    gi_copies = []

    def gi_send(j):
        src = gI.at[j, :, pl.ds(pl.multiple_of((1 - core) * CH, 128), CH)]
        gi_copies.append(copy_to(src, gIr.at[j], sibling))

    def gi_finish(j):
        gi_copies[j].wait_recv()
        gi_out[:, j * CH : (j + 1) * CH] = gIr[j] + gI[j, :, pl.ds(ccol, CH)]

    last = NCH - 1
    bzr = {}

    def bzr_first():
        for n, k, hop in ((0, 4, 2), (1, 3, 2), (2, -3, -2), (3, -2, -2)):
            i = zi(k)
            bzr[n] = copy_to(SB.at[i // HZ, i % HZ], rBz.at[n], zd(hop))

    def bzr_second():
        for n, k in ((0, 2), (1, 1), (2, -1)):
            i = zi(k)
            bzr[n].wait_recv()
            rBz[n] = rBz[n] + SB[i // HZ, i % HZ]
            bzr[4 + n] = copy_to(rBz.at[n], rBz.at[4 + n], zd(k))

    task(2, last, 2)
    bxr_send(0)
    task(0, last, 2)
    azr_send(0)
    lax.fori_loop(0, 4, transpose_tile, 0)
    bxr_send(1)
    gi_step(0, 0)
    gi_send(0)
    azr_send(1)
    for sub in range(2):
        total = G[2 + sub, :, 0]
        for d, length, rbuf in ((1, lfx, rBxf), (-1, lbx, rBxb)):
            if length:
                bxr[d, sub, length - 1].wait_recv()
                total = total + rbuf[length - 1, sub].astype(jnp.float32)
        SB[sub] = total
    bzr_first()
    if NCH > 1:
        gi_step(1, 0)
        gi_send(1)
    azr_send(2)
    if NCH > 2:
        gi_step(2, 0)
        gi_send(2)
    bzr_second()
    for sub in range(NSUB):
        xs = slice(sub * XS, (sub + 1) * XS)
        total = G[0, 0, xs]
        for d, length, rbuf in ((1, lfz, rAzf), (-1, lbz, rAzb)):
            if length:
                azr[d, sub, length - 1].wait_recv()
                total = total + rbuf[length - 1, sub].astype(jnp.float32)
        SA[xs] = total
    axr = [copy_to(SA.at[xi(k)], rAx.at[n], xd(k)) for n, k in enumerate(x_steps)]
    if NCH > 3:
        gi_step(3, 0)
        gi_send(3)
    for j in range(NCH):
        gi_finish(j)
    endA = SA[0]
    for n, c in enumerate(axr):
        c.wait_recv()
        endA = endA + rAx[n]
    endB = SB[0, 0]
    for n in range(3, 7):
        bzr[n].wait_recv()
        endB = endB + rBz[n]
    first = yh == 0
    finY[...] = jnp.where(first, endB, endA)
    last_copy = copy_to(finY, rY, dev_y)
    own = jnp.where(first, endA, endB)
    last_copy.wait_recv()
    gt_out[...] = own + rY[...]

    for c in started:
        c.wait_send()


def build(nz, ny, nx, F, C, total_images):
    lfx, lbx = chain_lengths(nx)
    lfz, lbz = chain_lengths(nz)
    hz, xs = nz // 2, nx // 2
    tm = hz * nx * R
    nch = C // CH
    tw = 2 * F - F // 128 * 128
    f32, bf16 = jnp.float32, jnp.bfloat16

    def chain(n, shape, dtype):
        return pltpu.VMEM((max(n, 1),) + shape, dtype)

    smem = pltpu.SMEM
    scratch = [
        pltpu.VMEM((R, F), bf16),
        smem((C * nz * ny * nx * 2 // 128,), jnp.int32),
        smem((nz * ny,), jnp.int32),
        smem((1,), f32),
        smem((1,), f32),
        smem((1,), f32),
        pltpu.VMEM((4, hz, nx, R, 2 * F), bf16),
        pltpu.VMEM((4, tw, tm), bf16),
        pltpu.VMEM((nch, 2 * F, 2 * CH), bf16),
        pltpu.VMEM((nch, 4, tm, 2 * CH), bf16),
        pltpu.VMEM((4, hz, nx, R, F), f32),
        pltpu.VMEM((nch, F, 2 * CH), f32),
        pltpu.VMEM((nch, F, CH), f32),
        pltpu.VMEM((4, tm, 128), jnp.int32),
        pltpu.VMEM((4, R, -(-F // 128) * 128), bf16),
        *[chain(n, (2, xs, R, F), WIRE_A) for n in (lfz, lbz, lfz, lbz)],
        *[chain(n, (2, hz, R, F), WIRE_B) for n in (lfx, lbx, lfx, lbx)],
        pltpu.VMEM((nx, R, F), f32),
        pltpu.VMEM((3, R, F), f32),
        pltpu.VMEM((2, hz, R, F), f32),
        pltpu.VMEM((7, R, F), f32),
        pltpu.VMEM((R, F), f32),
        pltpu.VMEM((R, F), f32),
        pltpu.SemaphoreType.DMA((140,)),
        pltpu.SemaphoreType.DMA((140,)),
        pltpu.SemaphoreType.DMA((nch + 6,)),
    ]
    vmem = pl.BlockSpec(memory_space=pltpu.VMEM)
    hbm = pl.BlockSpec(memory_space=pl.ANY)

    def body(images, texts, img_group, txt_group, temp, bias, loss_scale):
        gi, gt = pl.pallas_call(
            functools.partial(kernel, (nz, ny, nx, F, C, total_images)),
            out_shape=(pltpu.VMEM((F, C), f32), pltpu.VMEM((R, F), f32)),
            in_specs=[hbm] * 7,
            out_specs=(vmem, vmem),
            scratch_shapes=scratch,
            compiler_params=pltpu.CompilerParams(
                collective_id=0, has_side_effects=True, vmem_limit_bytes=56 * 1024 * 1024
            ),
        )(images.T, texts, img_group, txt_group, temp.reshape(1), bias.reshape(1), loss_scale.reshape(1))
        return gi.T, gt

    return body


def solution(mesh):
    body = build(NZ, NY, NX, 576, 1024, 131072)
    in_specs = (P("blk", "feat"), P("blk", "feat"), P(), P(), P(), P(), P())
    out_specs = (P("blk", "feat"), P("blk", "feat"))
    return jax.shard_map(body, mesh=mesh, in_specs=in_specs, out_specs=out_specs, check_vma=False)
```

```python
import functools

import jax
import jax.numpy as jnp
from jax import lax
from jax.experimental import pallas as pl
from jax.experimental.pallas import tpu as pltpu
from jax.sharding import PartitionSpec as P

MESH = pl.DeviceIdType.MESH
NZ, NY, NX = 8, 2, 4
R = 16
CH = 256
WIRE_A = jnp.bfloat16
WIRE_B = jnp.bfloat16


def chain_lengths(n):
    return n // 2, (n - 1) // 2


def near_first(n):
    lf, lb = chain_lengths(n)
    return sorted(range(-lf, lb + 1), key=lambda k: (abs(k), k))


def kernel(
    cfg,
    img_ref, txt_hbm, ig_hbm, tg_hbm, temp_ref, bias_ref, scale_ref,
    gi_out, gt_out,
    txt_ref, ig_ref, tg_ref,
    T, TT, I, W, G, gI, gIr, tgv, Y,
    sAzf, sAzb, rAzf, rAzb, sBxf, sBxb, rBxf, rBxb,
    SA, rAx, SB, sB1, rB1, rBz, finY, rY,
    send, recv, loc,
):
    nz, ny, nx, F, C, total_images = cfg
    NCH = C // CH
    HZ = nz // 2
    TM = HZ * nx * R
    W2 = 2 * CH
    ZO, XO = near_first(nz), near_first(nx)
    lfz, lbz = chain_lengths(nz)
    lfx, lbx = chain_lengths(nx)

    def norm(k, n):
        return k - n if k > (n - 1) // 2 else k

    def zi(k):
        return ZO.index(norm(k, nz))

    def xi(k):
        return XO.index(norm(k, nx))

    blk = lax.axis_index("blk")
    feat = lax.axis_index("feat")
    core = lax.rem(blk, 2)
    x = lax.rem(blk // 2, nx)
    yh = lax.rem(blk // (2 * nx), ny)
    z = blk // (2 * nx * ny)
    step_dir = 1 - 2 * core

    def at(z_, yh_, x_, core_, feat_):
        return (((z_ * ny + yh_) * nx + x_) * 2 + core_, feat_)

    def zz(k):
        return lax.rem(z + step_dir * k + 2 * nz, nz)

    def xx(k):
        return lax.rem(x + step_dir * k + 2 * nx, nx)

    sibling = at(z, yh, x, 1 - core, feat)
    dev_f = at(z, yh, x, core, 1 - feat)
    dev_y = at(z, 1 - yh, x, core, feat)
    dev_d = at(z, 1 - yh, x, core, 1 - feat)
    zf, zb = at(zz(1), yh, x, core, feat), at(zz(-1), yh, x, core, feat)

    def xd(k):
        return at(z, yh, xx(k), core, feat)

    def zd(k):
        return at(zz(k), yh, x, core, feat)

    x_steps = [k for k in (1, -1, 2) if k < nx and (k != -1 or nx > 2)]
    txt_copy = pltpu.make_async_copy(txt_hbm, txt_ref, loc.at[NCH])
    txt_copy.start()
    small = [
        pltpu.make_async_copy(src, dst, loc.at[NCH + 1 + n])
        for n, (src, dst) in enumerate(
            ((ig_hbm, ig_ref), (tg_hbm, tg_ref))
        )
    ]
    for c in small:
        c.start()
    barrier = pltpu.get_barrier_semaphore()
    partners = [sibling, dev_f, dev_y, dev_d, zf, zb, zd(2), zd(-2)] + [xd(k) for k in x_steps]
    for dev in partners:
        pl.semaphore_signal(barrier, inc=1, device_id=dev, device_id_type=MESH)

    ccol = pl.multiple_of(core * CH, 128)
    frow = pl.multiple_of(feat * F, 16)
    orow = pl.multiple_of((1 - feat) * F, 16)

    def img_src(j):
        return img_ref.at[:, pl.ds(j * CH, CH)]

    def img_dst(j):
        return I.at[j, pl.ds(frow, F), pl.ds(ccol, CH)]

    own_copies = [pltpu.make_async_copy(img_src(j), img_dst(j), loc.at[j]) for j in range(NCH)]
    for c in own_copies:
        c.start()
    me = yh * 2 + feat
    txt_copy.wait()
    Y[me, :, 0:F] = txt_ref[...]
    for c in small:
        c.wait()
    for i, kz in enumerate(ZO):
        t, a = divmod(i, HZ)
        for h in range(2):
            group = jnp.full((nx * R, 128), tg_ref[zz(kz) * ny + h], jnp.int32)
            tgv[2 * h + t, a * nx * R : (a + 1) * nx * R, :] = group
    G[...] = jnp.zeros_like(G)

    pl.semaphore_wait(barrier, len(partners))

    count = [0]
    started = []

    def copy_to(src, dst, dev):
        i = count[0]
        count[0] += 1
        c = pltpu.make_async_remote_copy(
            src_ref=src, dst_ref=dst, send_sem=send.at[i], recv_sem=recv.at[i], device_id=dev, device_id_type=MESH
        )
        c.start()
        started.append(c)
        return c

    y_copies = [copy_to(Y.at[me], Y.at[me], dev) for dev in (dev_f, dev_y, dev_d)]
    img_copies = [copy_to(img_src(j), img_dst(j), dev_f) for j in range(NCH)]
    sib_copies = [copy_to(img_src(j), img_dst(j), sibling) for j in range(NCH)]
    fwd_copies = {}

    def forward_images(j):
        if j < NCH:
            img_copies[j].wait_recv()
            ref = I.at[j, pl.ds(orow, F), pl.ds(ccol, CH)]
            fwd_copies[j] = copy_to(ref, ref, sibling)

    ready = set()

    def images_ready(j):
        if j < NCH and j not in ready:
            ready.add(j)
            own_copies[j].wait()
            sib_copies[j].wait_recv()
            fwd_copies[j].wait_recv()

    temp, bias = temp_ref[()], bias_ref[()]
    factor = -(scale_ref[()] * temp / total_images)

    def task(m, j, n=1):
        raw = jnp.dot(T[pl.ds(m, n)].reshape(n * TM, 2 * F), I[j], preferred_element_type=jnp.float32)
        tg = tgv[pl.ds(m, n)].reshape(n * TM, 128)
        parts = []
        for q in range(W2 // 128):
            per = CH // 128
            group = ig_ref[(blk - core + q // per) * (C // 128) + j * per + q % per]
            logit = temp * raw[:, q * 128 : (q + 1) * 128] + bias
            same = tg == group
            p = 1.0 / (1.0 + jnp.exp(jnp.where(same, logit, -logit)))
            parts.append((jnp.where(same, factor, -factor) * p).astype(jnp.bfloat16))
        w = jnp.concatenate(parts, axis=1)
        W[j, pl.ds(m, n)] = w.reshape(n, TM, W2)
        part = lax.dot_general(
            w, I[j, pl.ds(frow, F), :], (((1,), (1,)), ((), ())), preferred_element_type=jnp.float32
        )
        G[pl.ds(m, n)] = G[pl.ds(m, n)] + part.reshape(n, HZ, nx, R, F)

    def slot(h, kz, kx):
        i = zi(kz)
        return T.at[2 * h + i // HZ, i % HZ, xi(kx)]

    for c in y_copies:
        c.wait_recv()
    for h in range(2):
        T[2 * h, 0, 0] = jnp.concatenate([Y[2 * h, :, 0:F], Y[2 * h + 1, :, 0:F]], axis=1)

    az, bz, bx, ax = {}, {}, {}, {}

    def z_send(store, h, kx, s):
        if s < lfz:
            store[kx, 1, s] = copy_to(slot(h, -s, kx), slot(h, -s - 1, kx), zf)
        if s < lbz:
            store[kx, -1, s] = copy_to(slot(h, s, kx), slot(h, s + 1, kx), zb)

    def z_wait(store, kx, s):
        for d in (1, -1):
            if (kx, d, s) in store:
                store[kx, d, s].wait_recv()

    def bx_send(kz):
        if kz in bx or kz not in ZO:
            return
        bx[kz] = [copy_to(slot(1, kz, 0), slot(1, kz, -1), xd(1))]
        if lbx:
            bx[kz].append(copy_to(slot(1, kz, 0), slot(1, kz, 1), xd(-1)))

    bx2 = {}

    def bx_fwd(kz):
        if kz in bx2 or kz not in ZO or lfx < 2:
            return
        bx[kz][0].wait_recv()
        bx2[kz] = copy_to(slot(1, kz, -1), slot(1, kz, -2), xd(1))

    def bx_fin(kz):
        if lfx < 2:
            bx[kz][0].wait_recv()
        else:
            bx2[kz].wait_recv()
        for c in bx[kz][1:]:
            c.wait_recv()

    def bz_send(k, frm=0):
        bz[k] = copy_to(slot(1, frm, 0), slot(1, frm - (k - SIGN[k] * abs(frm)), 0), zd(k - SIGN[k] * abs(frm)))

    SIGN = {1: 1, 2: 1, 3: 1, 4: 1, -1: -1, -2: -1, -3: -1}
    for k in (1, -1, 2, -2):
        bz_send(k)
    for k in x_steps:
        ax[k] = copy_to(slot(0, 0, 0), slot(0, 0, -k), xd(k))
    z_send(az, 0, 0, 0)
    bx_send(0)
    others = [norm(-k, nx) for k in x_steps]

    def az_on(kxs, s):
        for kx in kxs:
            z_wait(az, kx, s - 1)
            z_send(az, 0, kx, s)

    def bz_got(*ks):
        for k in ks:
            bz[k].wait_recv()
        for k in ks:
            bx_send(-k)

    bz_got(1, -1)
    for k in x_steps[:2]:
        ax[k].wait_recv()
        z_send(az, 0, norm(-k, nx), 0)
    bz[2].wait_recv()
    bz_send(4, -2)
    bz_send(3, -2)
    bz[-2].wait_recv()
    bz_send(-3, 2)
    az_on([0], 1)
    bx_send(-2)
    bx_send(2)
    for k in x_steps[2:]:
        ax[k].wait_recv()
        z_send(az, 0, norm(-k, nx), 0)
    bx_fwd(0)
    az_on(others[:2], 1)
    bx_fwd(-1)
    bx_fwd(1)
    az_on([0], 2)
    az_on(others[2:], 1)
    bz_got(3, -3, 4)
    bx_fwd(-2)
    forward_images(0)
    az_on(others[:2], 2)
    az_on([0], 3)
    az_on(others[2:], 2)
    for kz in ZO[:HZ]:
        bx_fin(kz)
    images_ready(0)
    task(2, 0)
    bx_fwd(2)
    bx_fwd(-3)
    bx_fwd(3)
    bx_fwd(-4)
    az_on(others[:2], 3)
    az_on(others[2:], 3)
    task(0, 0)
    forward_images(1)
    for kz in ZO[HZ:]:
        bx_fin(kz)
    task(3, 0)
    images_ready(1)
    task(2, 1, 2)
    for kx in [0] + others:
        z_wait(az, kx, lfz - 1)
    forward_images(2)
    task(1, 0)
    task(0, 1, 2)
    images_ready(2)
    forward_images(3)
    task(0, 2, 4)
    images_ready(3)

    NSUB = 2
    XS = nx // NSUB

    def azr_send(s):
        for sub in range(NSUB):
            xs = slice(sub * XS, (sub + 1) * XS)

            def block(k):
                i = zi(k)
                return G[i // HZ, i % HZ, xs]

            def put(key, val, sbuf, rbuf, dev):
                sbuf[key[1], sub] = val.astype(sbuf.dtype)
                azr[key[0], sub, key[1]] = copy_to(sbuf.at[key[1], sub], rbuf.at[key[1], sub], dev)

            if s == 0:
                put((1, 0), block(4), sAzf, rAzf, zd(2))
                put((1, 1), block(3), sAzf, rAzf, zf)
            elif s == 1:
                azr[1, sub, 0].wait_recv()
                azr[1, sub, 1].wait_recv()
                val = block(2) + rAzf[0, sub].astype(jnp.float32) + rAzf[1, sub].astype(jnp.float32)
                put((1, 2), val, sAzf, rAzf, zf)
            else:
                azr[1, sub, 2].wait_recv()
                put((1, 3), block(1) + rAzf[2, sub].astype(jnp.float32), sAzf, rAzf, zf)
            val = block(s - 3)
            if s > 0:
                azr[-1, sub, s - 1].wait_recv()
                val = val + rAzb[s - 1, sub].astype(jnp.float32)
            put((-1, s), val, sAzb, rAzb, zb)

    azr = {}
    bxr = {}

    def bxr_send(s):
        for sub in range(2):
            for d, length, sbuf, rbuf in ((1, lfx, sBxf, rBxf), (-1, lbx, sBxb, rBxb)):
                if s >= length:
                    continue
                if s > 0:
                    bxr[d, sub, s - 1].wait_recv()
                val = G[2 + sub, :, xi(d * (length - s))]
                if s > 0:
                    val = val + rbuf[s - 1, sub].astype(jnp.float32)
                sbuf[s, sub] = val.astype(sbuf.dtype)
                bxr[d, sub, s] = copy_to(sbuf.at[s, sub], rbuf.at[s, sub], xd(d))

    LO = F // 128 * 128
    TW = 2 * F - LO

    def transpose_tile(m, c):
        rows = T[m].reshape(TM, 2 * F)
        own = jnp.where(feat == 0, rows[:, 0:TW], rows[:, LO : LO + TW])
        TT[m] = own.T
        return c

    def gi_step(j, c):
        off = pl.multiple_of(feat * (F - LO), 16)
        total = None
        for m in range(4):
            part = jnp.dot(TT[m, pl.ds(off, F), :], W[j, m], preferred_element_type=jnp.float32)
            total = part if total is None else total + part
        gI[j] = total
        return c

    gi_copies = []

    def gi_send(j):
        src = gI.at[j, :, pl.ds(pl.multiple_of((1 - core) * CH, 128), CH)]
        gi_copies.append(copy_to(src, gIr.at[j], sibling))

    def gi_finish(j):
        gi_copies[j].wait_recv()
        gi_out[:, j * CH : (j + 1) * CH] = gIr[j] + gI[j, :, pl.ds(ccol, CH)]

    last = NCH - 1
    bzr = {}

    def bzr_first():
        for n, k, hop in ((0, 4, 2), (1, 3, 2), (2, -3, -2), (3, -2, -2)):
            i = zi(k)
            sB1[n] = SB[i // HZ, i % HZ].astype(sB1.dtype)
            bzr[n] = copy_to(sB1.at[n], rB1.at[n], zd(hop))

    def bzr_second():
        for n, k in ((0, 2), (1, 1), (2, -1)):
            i = zi(k)
            bzr[n].wait_recv()
            rBz[n] = rB1[n].astype(jnp.float32) + SB[i // HZ, i % HZ]
            bzr[4 + n] = copy_to(rBz.at[n], rBz.at[4 + n], zd(k))

    task(2, last, 2)
    bxr_send(0)
    task(0, last, 2)
    azr_send(0)
    lax.fori_loop(0, 4, transpose_tile, 0)
    bxr_send(1)
    gi_step(0, 0)
    gi_send(0)
    azr_send(1)
    for sub in range(2):
        total = G[2 + sub, :, 0]
        for d, length, rbuf in ((1, lfx, rBxf), (-1, lbx, rBxb)):
            if length:
                bxr[d, sub, length - 1].wait_recv()
                total = total + rbuf[length - 1, sub].astype(jnp.float32)
        SB[sub] = total
    bzr_first()
    if NCH > 1:
        gi_step(1, 0)
        gi_send(1)
    azr_send(2)
    if NCH > 2:
        gi_step(2, 0)
        gi_send(2)
    bzr_second()
    for sub in range(NSUB):
        xs = slice(sub * XS, (sub + 1) * XS)
        total = G[0, 0, xs]
        for d, length, rbuf in ((1, lfz, rAzf), (-1, lbz, rAzb)):
            if length:
                azr[d, sub, length - 1].wait_recv()
                total = total + rbuf[length - 1, sub].astype(jnp.float32)
        SA[xs] = total
    axr = [copy_to(SA.at[xi(k)], rAx.at[n], xd(k)) for n, k in enumerate(x_steps)]
    if NCH > 3:
        gi_step(3, 0)
        gi_send(3)
    for j in range(NCH):
        gi_finish(j)
    endA = SA[0]
    for n, c in enumerate(axr):
        c.wait_recv()
        endA = endA + rAx[n]
    endB = SB[0, 0]
    bzr[3].wait_recv()
    endB = endB + rB1[3].astype(jnp.float32)
    for n in range(4, 7):
        bzr[n].wait_recv()
        endB = endB + rBz[n]
    first = yh == 0
    finY[...] = jnp.where(first, endB, endA)
    last_copy = copy_to(finY, rY, dev_y)
    own = jnp.where(first, endA, endB)
    last_copy.wait_recv()
    gt_out[...] = own + rY[...]

    for c in started:
        c.wait_send()


def build(nz, ny, nx, F, C, total_images):
    lfx, lbx = chain_lengths(nx)
    lfz, lbz = chain_lengths(nz)
    hz, xs = nz // 2, nx // 2
    tm = hz * nx * R
    nch = C // CH
    tw = 2 * F - F // 128 * 128
    f32, bf16 = jnp.float32, jnp.bfloat16

    def chain(n, shape, dtype):
        return pltpu.VMEM((max(n, 1),) + shape, dtype)

    smem = pltpu.SMEM
    scratch = [
        pltpu.VMEM((R, F), bf16),
        smem((C * nz * ny * nx * 2 // 128,), jnp.int32),
        smem((nz * ny,), jnp.int32),
        pltpu.VMEM((4, hz, nx, R, 2 * F), bf16),
        pltpu.VMEM((4, tw, tm), bf16),
        pltpu.VMEM((nch, 2 * F, 2 * CH), bf16),
        pltpu.VMEM((nch, 4, tm, 2 * CH), bf16),
        pltpu.VMEM((4, hz, nx, R, F), f32),
        pltpu.VMEM((nch, F, 2 * CH), f32),
        pltpu.VMEM((nch, F, CH), f32),
        pltpu.VMEM((4, tm, 128), jnp.int32),
        pltpu.VMEM((4, R, -(-F // 128) * 128), bf16),
        *[chain(n, (2, xs, R, F), WIRE_A) for n in (lfz, lbz, lfz, lbz)],
        *[chain(n, (2, hz, R, F), WIRE_B) for n in (lfx, lbx, lfx, lbx)],
        pltpu.VMEM((nx, R, F), f32),
        pltpu.VMEM((3, R, F), f32),
        pltpu.VMEM((2, hz, R, F), f32),
        pltpu.VMEM((4, R, F), WIRE_B),
        pltpu.VMEM((4, R, F), WIRE_B),
        pltpu.VMEM((7, R, F), f32),
        pltpu.VMEM((R, F), f32),
        pltpu.VMEM((R, F), f32),
        pltpu.SemaphoreType.DMA((140,)),
        pltpu.SemaphoreType.DMA((140,)),
        pltpu.SemaphoreType.DMA((nch + 3,)),
    ]
    vmem = pl.BlockSpec(memory_space=pltpu.VMEM)
    hbm = pl.BlockSpec(memory_space=pl.ANY)

    def body(images, texts, img_group, txt_group, temp, bias, loss_scale):
        gi, gt = pl.pallas_call(
            functools.partial(kernel, (nz, ny, nx, F, C, total_images)),
            out_shape=(pltpu.VMEM((F, C), f32), pltpu.VMEM((R, F), f32)),
            in_specs=[hbm] * 4 + [pl.BlockSpec(memory_space=pltpu.SMEM)] * 3,
            out_specs=(vmem, vmem),
            scratch_shapes=scratch,
            compiler_params=pltpu.CompilerParams(
                collective_id=0, has_side_effects=True, vmem_limit_bytes=56 * 1024 * 1024
            ),
        )(images.T, texts, img_group, txt_group, temp, bias, loss_scale)
        return gi.T, gt

    return body


def solution(mesh):
    body = build(NZ, NY, NX, 576, 1024, 131072)
    in_specs = (P("blk", "feat"), P("blk", "feat"), P(), P(), P(), P(), P())
    out_specs = (P("blk", "feat"), P("blk", "feat"))
    return jax.shard_map(body, mesh=mesh, in_specs=in_specs, out_specs=out_specs, check_vma=False)
```

```python
import functools

import jax
import jax.numpy as jnp
from jax import lax
from jax.experimental import pallas as pl
from jax.experimental.pallas import tpu as pltpu
from jax.sharding import PartitionSpec as P

MESH = pl.DeviceIdType.MESH
NZ, NY, NX = 8, 2, 4
R = 16
CH = 256
WIRE_A = jnp.bfloat16
WIRE_B = jnp.bfloat16


def chain_lengths(n):
    return n // 2, (n - 1) // 2


def near_first(n):
    lf, lb = chain_lengths(n)
    return sorted(range(-lf, lb + 1), key=lambda k: (abs(k), k))


def kernel(
    cfg,
    img_ref, txt_hbm, ig_hbm, tg_hbm, temp_ref, bias_ref, scale_ref,
    gi_out, gt_out,
    txt_ref, ig_ref, tg_ref,
    T, TT, I, W, G, gI, gIr, tgv, Y,
    sAzf, sAzb, rAzf, rAzb, sBxf, sBxb, rBxf, rBxb,
    SA, rAx, SB, sB1, rB1, rBz, finY, rY,
    send, recv, loc,
):
    nz, ny, nx, F, C, total_images = cfg
    NCH = C // CH
    HZ = nz // 2
    TM = HZ * nx * R
    W2 = 2 * CH
    ZO, XO = near_first(nz), near_first(nx)
    lfz, lbz = chain_lengths(nz)
    lfx, lbx = chain_lengths(nx)

    def norm(k, n):
        return k - n if k > (n - 1) // 2 else k

    def zi(k):
        return ZO.index(norm(k, nz))

    def xi(k):
        return XO.index(norm(k, nx))

    blk = lax.axis_index("blk")
    feat = lax.axis_index("feat")
    core = lax.rem(blk, 2)
    x = lax.rem(blk // 2, nx)
    yh = lax.rem(blk // (2 * nx), ny)
    z = blk // (2 * nx * ny)
    step_dir = 1 - 2 * core

    def at(z_, yh_, x_, core_, feat_):
        return (((z_ * ny + yh_) * nx + x_) * 2 + core_, feat_)

    def zz(k):
        return lax.rem(z + step_dir * k + 2 * nz, nz)

    def xx(k):
        return lax.rem(x + step_dir * k + 2 * nx, nx)

    sibling = at(z, yh, x, 1 - core, feat)
    dev_f = at(z, yh, x, core, 1 - feat)
    dev_y = at(z, 1 - yh, x, core, feat)
    dev_d = at(z, 1 - yh, x, core, 1 - feat)
    zf, zb = at(zz(1), yh, x, core, feat), at(zz(-1), yh, x, core, feat)

    def xd(k):
        return at(z, yh, xx(k), core, feat)

    def zd(k):
        return at(zz(k), yh, x, core, feat)

    x_steps = [k for k in (1, -1, 2) if k < nx and (k != -1 or nx > 2)]
    txt_copy = pltpu.make_async_copy(txt_hbm, txt_ref, loc.at[NCH])
    txt_copy.start()
    small = [
        pltpu.make_async_copy(src, dst, loc.at[NCH + 1 + n])
        for n, (src, dst) in enumerate(
            ((ig_hbm, ig_ref), (tg_hbm, tg_ref))
        )
    ]
    for c in small:
        c.start()
    barrier = pltpu.get_barrier_semaphore()
    partners = [sibling, dev_f, dev_y, dev_d, zf, zb, zd(2), zd(-2)] + [xd(k) for k in x_steps]
    for dev in partners:
        pl.semaphore_signal(barrier, inc=1, device_id=dev, device_id_type=MESH)

    ccol = pl.multiple_of(core * CH, 128)
    frow = pl.multiple_of(feat * F, 16)
    orow = pl.multiple_of((1 - feat) * F, 16)

    def img_src(j):
        return img_ref.at[:, pl.ds(j * CH, CH)]

    def img_dst(j):
        return I.at[j, pl.ds(frow, F), pl.ds(ccol, CH)]

    own_copies = [pltpu.make_async_copy(img_src(j), img_dst(j), loc.at[j]) for j in range(NCH)]
    for c in own_copies:
        c.start()
    me = yh * 2 + feat
    txt_copy.wait()
    Y[me, :, 0:F] = txt_ref[...]
    for c in small:
        c.wait()
    for i, kz in enumerate(ZO):
        t, a = divmod(i, HZ)
        for h in range(2):
            group = jnp.full((nx * R, 128), tg_ref[zz(kz) * ny + h], jnp.int32)
            tgv[2 * h + t, a * nx * R : (a + 1) * nx * R, :] = group
    G[...] = jnp.zeros_like(G)

    pl.semaphore_wait(barrier, len(partners))

    count = [0]
    started = []

    def copy_to(src, dst, dev):
        i = count[0]
        count[0] += 1
        c = pltpu.make_async_remote_copy(
            src_ref=src, dst_ref=dst, send_sem=send.at[i], recv_sem=recv.at[i], device_id=dev, device_id_type=MESH
        )
        c.start()
        started.append(c)
        return c

    y_copies = [copy_to(Y.at[me], Y.at[me], dev) for dev in (dev_f, dev_y, dev_d)]
    img_copies = [copy_to(img_src(j), img_dst(j), dev_f) for j in range(NCH)]
    sib_copies = [copy_to(img_src(j), img_dst(j), sibling) for j in range(NCH)]
    fwd_copies = {}

    def forward_images(j):
        if j < NCH:
            img_copies[j].wait_recv()
            ref = I.at[j, pl.ds(orow, F), pl.ds(ccol, CH)]
            fwd_copies[j] = copy_to(ref, ref, sibling)

    ready = set()

    def images_ready(j):
        if j < NCH and j not in ready:
            ready.add(j)
            own_copies[j].wait()
            sib_copies[j].wait_recv()
            fwd_copies[j].wait_recv()

    temp, bias = temp_ref[()], bias_ref[()]
    factor = -(scale_ref[()] * temp / total_images)

    def task(m, j, n=1):
        raw = jnp.dot(T[pl.ds(m, n)].reshape(n * TM, 2 * F), I[j], preferred_element_type=jnp.float32)
        tg = tgv[pl.ds(m, n)].reshape(n * TM, 128)
        parts = []
        for q in range(W2 // 128):
            per = CH // 128
            group = ig_ref[(blk - core + q // per) * (C // 128) + j * per + q % per]
            logit = temp * raw[:, q * 128 : (q + 1) * 128] + bias
            same = tg == group
            p = 1.0 / (1.0 + jnp.exp(jnp.where(same, logit, -logit)))
            parts.append((jnp.where(same, factor, -factor) * p).astype(jnp.bfloat16))
        w = jnp.concatenate(parts, axis=1)
        W[j, pl.ds(m, n)] = w.reshape(n, TM, W2)
        part = lax.dot_general(
            w, I[j, pl.ds(frow, F), :], (((1,), (1,)), ((), ())), preferred_element_type=jnp.float32
        )
        G[pl.ds(m, n)] = G[pl.ds(m, n)] + part.reshape(n, HZ, nx, R, F)

    def slot(h, kz, kx):
        i = zi(kz)
        return T.at[2 * h + i // HZ, i % HZ, xi(kx)]

    for c in y_copies:
        c.wait_recv()
    for h in range(2):
        T[2 * h, 0, 0] = jnp.concatenate([Y[2 * h, :, 0:F], Y[2 * h + 1, :, 0:F]], axis=1)

    az, bz, bx, ax = {}, {}, {}, {}

    def z_send(store, h, kx, s):
        if s < lfz:
            store[kx, 1, s] = copy_to(slot(h, -s, kx), slot(h, -s - 1, kx), zf)
        if s < lbz:
            store[kx, -1, s] = copy_to(slot(h, s, kx), slot(h, s + 1, kx), zb)

    def z_wait(store, kx, s):
        for d in (1, -1):
            if (kx, d, s) in store:
                store[kx, d, s].wait_recv()

    def bx_send(kz):
        if kz in bx or kz not in ZO:
            return
        bx[kz] = [copy_to(slot(1, kz, 0), slot(1, kz, -1), xd(1))]
        if lbx:
            bx[kz].append(copy_to(slot(1, kz, 0), slot(1, kz, 1), xd(-1)))

    bx2 = {}

    def bx_fwd(kz):
        if kz in bx2 or kz not in ZO or lfx < 2:
            return
        bx[kz][0].wait_recv()
        bx2[kz] = copy_to(slot(1, kz, -1), slot(1, kz, -2), xd(1))

    def bx_fin(kz):
        if lfx < 2:
            bx[kz][0].wait_recv()
        else:
            bx2[kz].wait_recv()
        for c in bx[kz][1:]:
            c.wait_recv()

    def bz_send(k, frm=0):
        bz[k] = copy_to(slot(1, frm, 0), slot(1, frm - (k - SIGN[k] * abs(frm)), 0), zd(k - SIGN[k] * abs(frm)))

    SIGN = {1: 1, 2: 1, 3: 1, 4: 1, -1: -1, -2: -1, -3: -1}
    for k in (1, -1, 2, -2):
        bz_send(k)
    for k in x_steps:
        ax[k] = copy_to(slot(0, 0, 0), slot(0, 0, -k), xd(k))
    z_send(az, 0, 0, 0)
    bx_send(0)
    others = [norm(-k, nx) for k in x_steps]

    def az_on(kxs, s):
        for kx in kxs:
            z_wait(az, kx, s - 1)
            z_send(az, 0, kx, s)

    def bz_got(*ks):
        for k in ks:
            bz[k].wait_recv()
        for k in ks:
            bx_send(-k)

    bz_got(1, -1)
    for k in x_steps[:2]:
        ax[k].wait_recv()
        z_send(az, 0, norm(-k, nx), 0)
    bz[2].wait_recv()
    bz_send(4, -2)
    bz_send(3, -2)
    bz[-2].wait_recv()
    bz_send(-3, 2)
    az_on([0], 1)
    bx_send(-2)
    bx_send(2)
    for k in x_steps[2:]:
        ax[k].wait_recv()
        z_send(az, 0, norm(-k, nx), 0)
    bx_fwd(0)
    az_on(others[:2], 1)
    bx_fwd(-1)
    bx_fwd(1)
    az_on([0], 2)
    az_on(others[2:], 1)
    bz_got(3, -3, 4)
    bx_fwd(-2)
    forward_images(0)
    az_on(others[:2], 2)
    az_on([0], 3)
    az_on(others[2:], 2)
    bx_fwd(2)
    bx_fwd(-3)
    bx_fwd(3)
    bx_fwd(-4)
    images_ready(0)
    task(0, 0)
    az_on(others[:2], 3)
    az_on(others[2:], 3)
    forward_images(1)
    for kz in ZO[:HZ]:
        bx_fin(kz)
    for kz in ZO[HZ:]:
        bx_fin(kz)
    task(2, 0, 2)
    images_ready(1)
    task(2, 1, 2)
    for kx in [0] + others:
        z_wait(az, kx, lfz - 1)
    forward_images(2)
    task(1, 0)
    task(0, 1, 2)
    images_ready(2)
    forward_images(3)
    task(0, 2, 4)
    images_ready(3)

    NSUB = 2
    XS = nx // NSUB

    def azr_send(s):
        for sub in range(NSUB):
            xs = slice(sub * XS, (sub + 1) * XS)

            def block(k):
                i = zi(k)
                return G[i // HZ, i % HZ, xs]

            def put(key, val, sbuf, rbuf, dev):
                sbuf[key[1], sub] = val.astype(sbuf.dtype)
                azr[key[0], sub, key[1]] = copy_to(sbuf.at[key[1], sub], rbuf.at[key[1], sub], dev)

            if s == 0:
                put((1, 0), block(4), sAzf, rAzf, zd(2))
                put((1, 1), block(3), sAzf, rAzf, zf)
            elif s == 1:
                azr[1, sub, 0].wait_recv()
                azr[1, sub, 1].wait_recv()
                val = block(2) + rAzf[0, sub].astype(jnp.float32) + rAzf[1, sub].astype(jnp.float32)
                put((1, 2), val, sAzf, rAzf, zf)
            else:
                azr[1, sub, 2].wait_recv()
                put((1, 3), block(1) + rAzf[2, sub].astype(jnp.float32), sAzf, rAzf, zf)
            val = block(s - 3)
            if s > 0:
                azr[-1, sub, s - 1].wait_recv()
                val = val + rAzb[s - 1, sub].astype(jnp.float32)
            put((-1, s), val, sAzb, rAzb, zb)

    azr = {}
    bxr = {}

    def bxr_send(s):
        for sub in range(2):
            for d, length, sbuf, rbuf in ((1, lfx, sBxf, rBxf), (-1, lbx, sBxb, rBxb)):
                if s >= length:
                    continue
                if s > 0:
                    bxr[d, sub, s - 1].wait_recv()
                val = G[2 + sub, :, xi(d * (length - s))]
                if s > 0:
                    val = val + rbuf[s - 1, sub].astype(jnp.float32)
                sbuf[s, sub] = val.astype(sbuf.dtype)
                bxr[d, sub, s] = copy_to(sbuf.at[s, sub], rbuf.at[s, sub], xd(d))

    LO = F // 128 * 128
    TW = 2 * F - LO

    def transpose_tile(m, c):
        rows = T[m].reshape(TM, 2 * F)
        own = jnp.where(feat == 0, rows[:, 0:TW], rows[:, LO : LO + TW])
        TT[m] = own.T
        return c

    def gi_step(j, c):
        off = pl.multiple_of(feat * (F - LO), 16)
        total = None
        for m in range(4):
            part = jnp.dot(TT[m, pl.ds(off, F), :], W[j, m], preferred_element_type=jnp.float32)
            total = part if total is None else total + part
        gI[j] = total
        return c

    gi_copies = []

    def gi_send(j):
        src = gI.at[j, :, pl.ds(pl.multiple_of((1 - core) * CH, 128), CH)]
        gi_copies.append(copy_to(src, gIr.at[j], sibling))

    def gi_finish(j):
        gi_copies[j].wait_recv()
        gi_out[:, j * CH : (j + 1) * CH] = gIr[j] + gI[j, :, pl.ds(ccol, CH)]

    last = NCH - 1
    bzr = {}

    def bzr_first():
        for n, k, hop in ((0, 4, 2), (1, 3, 2), (2, -3, -2), (3, -2, -2)):
            i = zi(k)
            sB1[n] = SB[i // HZ, i % HZ].astype(sB1.dtype)
            bzr[n] = copy_to(sB1.at[n], rB1.at[n], zd(hop))

    def bzr_second():
        for n, k in ((0, 2), (1, 1), (2, -1)):
            i = zi(k)
            bzr[n].wait_recv()
            rBz[n] = rB1[n].astype(jnp.float32) + SB[i // HZ, i % HZ]
            bzr[4 + n] = copy_to(rBz.at[n], rBz.at[4 + n], zd(k))

    task(2, last, 2)
    bxr_send(0)
    task(0, last, 2)
    azr_send(0)
    lax.fori_loop(0, 4, transpose_tile, 0)
    bxr_send(1)
    gi_step(0, 0)
    gi_send(0)
    azr_send(1)
    for sub in range(2):
        total = G[2 + sub, :, 0]
        for d, length, rbuf in ((1, lfx, rBxf), (-1, lbx, rBxb)):
            if length:
                bxr[d, sub, length - 1].wait_recv()
                total = total + rbuf[length - 1, sub].astype(jnp.float32)
        SB[sub] = total
    bzr_first()
    if NCH > 1:
        gi_step(1, 0)
        gi_send(1)
    azr_send(2)
    if NCH > 2:
        gi_step(2, 0)
        gi_send(2)
    bzr_second()
    for sub in range(NSUB):
        xs = slice(sub * XS, (sub + 1) * XS)
        total = G[0, 0, xs]
        for d, length, rbuf in ((1, lfz, rAzf), (-1, lbz, rAzb)):
            if length:
                azr[d, sub, length - 1].wait_recv()
                total = total + rbuf[length - 1, sub].astype(jnp.float32)
        SA[xs] = total
    axr = [copy_to(SA.at[xi(k)], rAx.at[n], xd(k)) for n, k in enumerate(x_steps)]
    if NCH > 3:
        gi_step(3, 0)
        gi_send(3)
    for j in range(NCH):
        gi_finish(j)
    endA = SA[0]
    for n, c in enumerate(axr):
        c.wait_recv()
        endA = endA + rAx[n]
    endB = SB[0, 0]
    bzr[3].wait_recv()
    endB = endB + rB1[3].astype(jnp.float32)
    for n in range(4, 7):
        bzr[n].wait_recv()
        endB = endB + rBz[n]
    first = yh == 0
    finY[...] = jnp.where(first, endB, endA)
    last_copy = copy_to(finY, rY, dev_y)
    own = jnp.where(first, endA, endB)
    last_copy.wait_recv()
    gt_out[...] = own + rY[...]

    for c in started:
        c.wait_send()


def build(nz, ny, nx, F, C, total_images):
    lfx, lbx = chain_lengths(nx)
    lfz, lbz = chain_lengths(nz)
    hz, xs = nz // 2, nx // 2
    tm = hz * nx * R
    nch = C // CH
    tw = 2 * F - F // 128 * 128
    f32, bf16 = jnp.float32, jnp.bfloat16

    def chain(n, shape, dtype):
        return pltpu.VMEM((max(n, 1),) + shape, dtype)

    smem = pltpu.SMEM
    scratch = [
        pltpu.VMEM((R, F), bf16),
        smem((C * nz * ny * nx * 2 // 128,), jnp.int32),
        smem((nz * ny,), jnp.int32),
        pltpu.VMEM((4, hz, nx, R, 2 * F), bf16),
        pltpu.VMEM((4, tw, tm), bf16),
        pltpu.VMEM((nch, 2 * F, 2 * CH), bf16),
        pltpu.VMEM((nch, 4, tm, 2 * CH), bf16),
        pltpu.VMEM((4, hz, nx, R, F), f32),
        pltpu.VMEM((nch, F, 2 * CH), f32),
        pltpu.VMEM((nch, F, CH), f32),
        pltpu.VMEM((4, tm, 128), jnp.int32),
        pltpu.VMEM((4, R, -(-F // 128) * 128), bf16),
        *[chain(n, (2, xs, R, F), WIRE_A) for n in (lfz, lbz, lfz, lbz)],
        *[chain(n, (2, hz, R, F), WIRE_B) for n in (lfx, lbx, lfx, lbx)],
        pltpu.VMEM((nx, R, F), f32),
        pltpu.VMEM((3, R, F), f32),
        pltpu.VMEM((2, hz, R, F), f32),
        pltpu.VMEM((4, R, F), WIRE_B),
        pltpu.VMEM((4, R, F), WIRE_B),
        pltpu.VMEM((7, R, F), f32),
        pltpu.VMEM((R, F), f32),
        pltpu.VMEM((R, F), f32),
        pltpu.SemaphoreType.DMA((140,)),
        pltpu.SemaphoreType.DMA((140,)),
        pltpu.SemaphoreType.DMA((nch + 3,)),
    ]
    vmem = pl.BlockSpec(memory_space=pltpu.VMEM)
    hbm = pl.BlockSpec(memory_space=pl.ANY)

    def body(images, texts, img_group, txt_group, temp, bias, loss_scale):
        gi, gt = pl.pallas_call(
            functools.partial(kernel, (nz, ny, nx, F, C, total_images)),
            out_shape=(pltpu.VMEM((F, C), f32), pltpu.VMEM((R, F), f32)),
            in_specs=[hbm] * 4 + [pl.BlockSpec(memory_space=pltpu.SMEM)] * 3,
            out_specs=(vmem, vmem),
            scratch_shapes=scratch,
            compiler_params=pltpu.CompilerParams(
                collective_id=0, has_side_effects=True, vmem_limit_bytes=56 * 1024 * 1024
            ),
        )(images.T, texts, img_group, txt_group, temp, bias, loss_scale)
        return gi.T, gt

    return body


def solution(mesh):
    body = build(NZ, NY, NX, 576, 1024, 131072)
    in_specs = (P("blk", "feat"), P("blk", "feat"), P(), P(), P(), P(), P())
    out_specs = (P("blk", "feat"), P("blk", "feat"))
    return jax.shard_map(body, mesh=mesh, in_specs=in_specs, out_specs=out_specs, check_vma=False)
```

```python
import functools

import jax
import jax.numpy as jnp
from jax import lax
from jax.experimental import pallas as pl
from jax.experimental.pallas import tpu as pltpu
from jax.sharding import PartitionSpec as P

MESH = pl.DeviceIdType.MESH
NZ, NY, NX = 8, 2, 4
R = 16
CH = 256
WIRE_A = jnp.bfloat16
WIRE_B = jnp.bfloat16


def chain_lengths(n):
    return n // 2, (n - 1) // 2


def near_first(n):
    lf, lb = chain_lengths(n)
    return sorted(range(-lf, lb + 1), key=lambda k: (abs(k), k))


def kernel(
    cfg,
    img_ref, txt_hbm, ig_hbm, tg_hbm, temp_ref, bias_ref, scale_ref,
    gi_out, gt_out,
    txt_ref, ig_ref, tg_ref,
    T, TT, I, W, G, gI, gIr, tgv, Y,
    sAzf, sAzb, rAzf, rAzb, sBxf, sBxb, rBxf, rBxb,
    SA, rAx, SB, sB1, rB1, rBz, finY, rY,
    send, recv, loc,
):
    nz, ny, nx, F, C, total_images = cfg
    NCH = C // CH
    HZ = nz // 2
    TM = HZ * nx * R
    W2 = 2 * CH
    ZO, XO = near_first(nz), near_first(nx)
    lfz, lbz = chain_lengths(nz)
    lfx, lbx = chain_lengths(nx)

    def norm(k, n):
        return k - n if k > (n - 1) // 2 else k

    def zi(k):
        return ZO.index(norm(k, nz))

    def xi(k):
        return XO.index(norm(k, nx))

    blk = lax.axis_index("blk")
    feat = lax.axis_index("feat")
    core = lax.rem(blk, 2)
    x = lax.rem(blk // 2, nx)
    yh = lax.rem(blk // (2 * nx), ny)
    z = blk // (2 * nx * ny)
    step_dir = 1 - 2 * core

    def at(z_, yh_, x_, core_, feat_):
        return (((z_ * ny + yh_) * nx + x_) * 2 + core_, feat_)

    def zz(k):
        return lax.rem(z + step_dir * k + 2 * nz, nz)

    def xx(k):
        return lax.rem(x + step_dir * k + 2 * nx, nx)

    sibling = at(z, yh, x, 1 - core, feat)
    dev_f = at(z, yh, x, core, 1 - feat)
    dev_y = at(z, 1 - yh, x, core, feat)
    dev_d = at(z, 1 - yh, x, core, 1 - feat)
    zf, zb = at(zz(1), yh, x, core, feat), at(zz(-1), yh, x, core, feat)

    def xd(k):
        return at(z, yh, xx(k), core, feat)

    def zd(k):
        return at(zz(k), yh, x, core, feat)

    x_steps = [k for k in (1, -1, 2) if k < nx and (k != -1 or nx > 2)]
    txt_copy = pltpu.make_async_copy(txt_hbm, txt_ref, loc.at[NCH])
    txt_copy.start()
    small = [
        pltpu.make_async_copy(src, dst, loc.at[NCH + 1 + n])
        for n, (src, dst) in enumerate(
            ((ig_hbm, ig_ref), (tg_hbm, tg_ref))
        )
    ]
    for c in small:
        c.start()
    barrier = pltpu.get_barrier_semaphore()
    partners = [sibling, dev_f, dev_y, dev_d, zf, zb, zd(2), zd(-2)] + [xd(k) for k in x_steps]
    for dev in partners:
        pl.semaphore_signal(barrier, inc=1, device_id=dev, device_id_type=MESH)

    ccol = pl.multiple_of(core * CH, 128)
    frow = pl.multiple_of(feat * F, 16)
    orow = pl.multiple_of((1 - feat) * F, 16)

    def img_src(j):
        return img_ref.at[:, pl.ds(j * CH, CH)]

    def img_dst(j):
        return I.at[j, pl.ds(frow, F), pl.ds(ccol, CH)]

    own_copies = [pltpu.make_async_copy(img_src(j), img_dst(j), loc.at[j]) for j in range(NCH)]
    for c in own_copies:
        c.start()
    me = yh * 2 + feat
    txt_copy.wait()
    Y[me, :, 0:F] = txt_ref[...]
    for c in small:
        c.wait()
    for i, kz in enumerate(ZO):
        t, a = divmod(i, HZ)
        for h in range(2):
            group = jnp.full((nx * R, 128), tg_ref[zz(kz) * ny + h], jnp.int32)
            tgv[2 * h + t, a * nx * R : (a + 1) * nx * R, :] = group
    G[...] = jnp.zeros_like(G)

    pl.semaphore_wait(barrier, len(partners))

    count = [0]
    started = []

    def copy_to(src, dst, dev):
        i = count[0]
        count[0] += 1
        c = pltpu.make_async_remote_copy(
            src_ref=src, dst_ref=dst, send_sem=send.at[i], recv_sem=recv.at[i], device_id=dev, device_id_type=MESH
        )
        c.start()
        started.append(c)
        return c

    y_copies = [copy_to(Y.at[me], Y.at[me], dev) for dev in (dev_f, dev_y, dev_d)]
    img_copies = [copy_to(img_src(j), img_dst(j), dev_f) for j in range(NCH)]
    sib_copies = [copy_to(img_src(j), img_dst(j), sibling) for j in range(NCH)]
    fwd_copies = {}

    def forward_images(j):
        if j < NCH:
            img_copies[j].wait_recv()
            ref = I.at[j, pl.ds(orow, F), pl.ds(ccol, CH)]
            fwd_copies[j] = copy_to(ref, ref, sibling)

    ready = set()

    def images_ready(j):
        if j < NCH and j not in ready:
            ready.add(j)
            own_copies[j].wait()
            sib_copies[j].wait_recv()
            fwd_copies[j].wait_recv()

    temp, bias = temp_ref[()], bias_ref[()]
    factor = -(scale_ref[()] * temp / total_images)

    def task(m, j, n=1):
        raw = jnp.dot(T[pl.ds(m, n)].reshape(n * TM, 2 * F), I[j], preferred_element_type=jnp.float32)
        tg = tgv[pl.ds(m, n)].reshape(n * TM, 128)
        parts = []
        for q in range(W2 // 128):
            per = CH // 128
            group = ig_ref[(blk - core + q // per) * (C // 128) + j * per + q % per]
            logit = temp * raw[:, q * 128 : (q + 1) * 128] + bias
            same = tg == group
            p = 1.0 / (1.0 + jnp.exp(jnp.where(same, logit, -logit)))
            parts.append((jnp.where(same, factor, -factor) * p).astype(jnp.bfloat16))
        w = jnp.concatenate(parts, axis=1)
        W[j, pl.ds(m, n)] = w.reshape(n, TM, W2)
        part = lax.dot_general(
            w, I[j, pl.ds(frow, F), :], (((1,), (1,)), ((), ())), preferred_element_type=jnp.float32
        )
        G[pl.ds(m, n)] = G[pl.ds(m, n)] + part.reshape(n, HZ, nx, R, F)

    def slot(h, kz, kx):
        i = zi(kz)
        return T.at[2 * h + i // HZ, i % HZ, xi(kx)]

    for c in y_copies:
        c.wait_recv()
    for h in range(2):
        T[2 * h, 0, 0] = jnp.concatenate([Y[2 * h, :, 0:F], Y[2 * h + 1, :, 0:F]], axis=1)

    az, bz, bx, ax = {}, {}, {}, {}

    def z_send(store, h, kx, s):
        if s < lfz:
            store[kx, 1, s] = copy_to(slot(h, -s, kx), slot(h, -s - 1, kx), zf)
        if s < lbz:
            store[kx, -1, s] = copy_to(slot(h, s, kx), slot(h, s + 1, kx), zb)

    def z_wait(store, kx, s):
        for d in (1, -1):
            if (kx, d, s) in store:
                store[kx, d, s].wait_recv()

    def bx_send(kz):
        if kz in bx or kz not in ZO:
            return
        bx[kz] = [copy_to(slot(1, kz, 0), slot(1, kz, -1), xd(1))]
        if lbx:
            bx[kz].append(copy_to(slot(1, kz, 0), slot(1, kz, 1), xd(-1)))

    bx2 = {}

    def bx_fwd(kz):
        if kz in bx2 or kz not in ZO or lfx < 2:
            return
        bx[kz][0].wait_recv()
        bx2[kz] = copy_to(slot(1, kz, -1), slot(1, kz, -2), xd(1))

    def bx_fin(kz):
        if lfx < 2:
            bx[kz][0].wait_recv()
        else:
            bx2[kz].wait_recv()
        for c in bx[kz][1:]:
            c.wait_recv()

    def bz_send(k, frm=0):
        bz[k] = copy_to(slot(1, frm, 0), slot(1, frm - (k - SIGN[k] * abs(frm)), 0), zd(k - SIGN[k] * abs(frm)))

    SIGN = {1: 1, 2: 1, 3: 1, 4: 1, -1: -1, -2: -1, -3: -1}
    for k in (1, -1, 2, -2):
        bz_send(k)
    for k in x_steps:
        ax[k] = copy_to(slot(0, 0, 0), slot(0, 0, -k), xd(k))
    z_send(az, 0, 0, 0)
    bx_send(0)
    others = [norm(-k, nx) for k in x_steps]

    def az_on(kxs, s):
        for kx in kxs:
            z_wait(az, kx, s - 1)
            z_send(az, 0, kx, s)

    def bz_got(*ks):
        for k in ks:
            bz[k].wait_recv()
        for k in ks:
            bx_send(-k)

    bz_got(1, -1)
    for k in x_steps[:2]:
        ax[k].wait_recv()
        z_send(az, 0, norm(-k, nx), 0)
    bz[2].wait_recv()
    bz_send(4, -2)
    bz_send(3, -2)
    bz[-2].wait_recv()
    bz_send(-3, 2)
    az_on([0], 1)
    bx_send(-2)
    bx_send(2)
    for k in x_steps[2:]:
        ax[k].wait_recv()
        z_send(az, 0, norm(-k, nx), 0)
    bx_fwd(0)
    az_on(others[:2], 1)
    bx_fwd(-1)
    bx_fwd(1)
    az_on([0], 2)
    az_on(others[2:], 1)
    bz_got(3, -3, 4)
    bx_fwd(-2)
    forward_images(0)
    az_on(others[:2], 2)
    az_on([0], 3)
    az_on(others[2:], 2)
    bx_fwd(2)
    bx_fwd(-3)
    bx_fwd(3)
    bx_fwd(-4)
    images_ready(0)
    task(0, 0)
    az_on(others[:2], 3)
    az_on(others[2:], 3)
    forward_images(1)
    for kz in ZO[:HZ]:
        bx_fin(kz)
    for kz in ZO[HZ:]:
        bx_fin(kz)
    task(2, 0, 2)
    images_ready(1)
    forward_images(2)
    task(2, 1, 2)
    images_ready(2)
    task(2, 2, 2)
    for kx in [0] + others:
        z_wait(az, kx, lfz - 1)
    task(1, 0)
    task(0, 1, 2)
    forward_images(3)
    task(0, 2, 2)
    images_ready(3)

    NSUB = 2
    XS = nx // NSUB

    def azr_send(s):
        for sub in range(NSUB):
            xs = slice(sub * XS, (sub + 1) * XS)

            def block(k):
                i = zi(k)
                return G[i // HZ, i % HZ, xs]

            def put(key, val, sbuf, rbuf, dev):
                sbuf[key[1], sub] = val.astype(sbuf.dtype)
                azr[key[0], sub, key[1]] = copy_to(sbuf.at[key[1], sub], rbuf.at[key[1], sub], dev)

            if s == 0:
                put((1, 0), block(4), sAzf, rAzf, zd(2))
                put((1, 1), block(3), sAzf, rAzf, zf)
            elif s == 1:
                azr[1, sub, 0].wait_recv()
                azr[1, sub, 1].wait_recv()
                val = block(2) + rAzf[0, sub].astype(jnp.float32) + rAzf[1, sub].astype(jnp.float32)
                put((1, 2), val, sAzf, rAzf, zf)
            else:
                azr[1, sub, 2].wait_recv()
                put((1, 3), block(1) + rAzf[2, sub].astype(jnp.float32), sAzf, rAzf, zf)
            val = block(s - 3)
            if s > 0:
                azr[-1, sub, s - 1].wait_recv()
                val = val + rAzb[s - 1, sub].astype(jnp.float32)
            put((-1, s), val, sAzb, rAzb, zb)

    azr = {}
    bxr = {}

    def bxr_send(s):
        for sub in range(2):
            for d, length, sbuf, rbuf in ((1, lfx, sBxf, rBxf), (-1, lbx, sBxb, rBxb)):
                if s >= length:
                    continue
                if s > 0:
                    bxr[d, sub, s - 1].wait_recv()
                val = G[2 + sub, :, xi(d * (length - s))]
                if s > 0:
                    val = val + rbuf[s - 1, sub].astype(jnp.float32)
                sbuf[s, sub] = val.astype(sbuf.dtype)
                bxr[d, sub, s] = copy_to(sbuf.at[s, sub], rbuf.at[s, sub], xd(d))

    LO = F // 128 * 128
    TW = 2 * F - LO

    def transpose_tile(m, c):
        rows = T[m].reshape(TM, 2 * F)
        own = jnp.where(feat == 0, rows[:, 0:TW], rows[:, LO : LO + TW])
        TT[m] = own.T
        return c

    def gi_step(j, c):
        off = pl.multiple_of(feat * (F - LO), 16)
        total = None
        for m in range(4):
            part = jnp.dot(TT[m, pl.ds(off, F), :], W[j, m], preferred_element_type=jnp.float32)
            total = part if total is None else total + part
        gI[j] = total
        return c

    gi_copies = []

    def gi_send(j):
        src = gI.at[j, :, pl.ds(pl.multiple_of((1 - core) * CH, 128), CH)]
        gi_copies.append(copy_to(src, gIr.at[j], sibling))

    def gi_finish(j):
        gi_copies[j].wait_recv()
        gi_out[:, j * CH : (j + 1) * CH] = gIr[j] + gI[j, :, pl.ds(ccol, CH)]

    last = NCH - 1
    bzr = {}

    def bzr_first():
        for n, k, hop in ((0, 4, 2), (1, 3, 2), (2, -3, -2), (3, -2, -2)):
            i = zi(k)
            sB1[n] = SB[i // HZ, i % HZ].astype(sB1.dtype)
            bzr[n] = copy_to(sB1.at[n], rB1.at[n], zd(hop))

    def bzr_second():
        for n, k in ((0, 2), (1, 1), (2, -1)):
            i = zi(k)
            bzr[n].wait_recv()
            rBz[n] = rB1[n].astype(jnp.float32) + SB[i // HZ, i % HZ]
            bzr[4 + n] = copy_to(rBz.at[n], rBz.at[4 + n], zd(k))

    task(2, last, 2)
    bxr_send(0)
    task(0, last, 2)
    azr_send(0)
    lax.fori_loop(0, 4, transpose_tile, 0)
    bxr_send(1)
    gi_step(0, 0)
    gi_send(0)
    azr_send(1)
    for sub in range(2):
        total = G[2 + sub, :, 0]
        for d, length, rbuf in ((1, lfx, rBxf), (-1, lbx, rBxb)):
            if length:
                bxr[d, sub, length - 1].wait_recv()
                total = total + rbuf[length - 1, sub].astype(jnp.float32)
        SB[sub] = total
    bzr_first()
    if NCH > 1:
        gi_step(1, 0)
        gi_send(1)
    azr_send(2)
    if NCH > 2:
        gi_step(2, 0)
        gi_send(2)
    bzr_second()
    for sub in range(NSUB):
        xs = slice(sub * XS, (sub + 1) * XS)
        total = G[0, 0, xs]
        for d, length, rbuf in ((1, lfz, rAzf), (-1, lbz, rAzb)):
            if length:
                azr[d, sub, length - 1].wait_recv()
                total = total + rbuf[length - 1, sub].astype(jnp.float32)
        SA[xs] = total
    axr = [copy_to(SA.at[xi(k)], rAx.at[n], xd(k)) for n, k in enumerate(x_steps)]
    if NCH > 3:
        gi_step(3, 0)
        gi_send(3)
    for j in range(NCH):
        gi_finish(j)
    endA = SA[0]
    for n, c in enumerate(axr):
        c.wait_recv()
        endA = endA + rAx[n]
    endB = SB[0, 0]
    bzr[3].wait_recv()
    endB = endB + rB1[3].astype(jnp.float32)
    for n in range(4, 7):
        bzr[n].wait_recv()
        endB = endB + rBz[n]
    first = yh == 0
    finY[...] = jnp.where(first, endB, endA)
    last_copy = copy_to(finY, rY, dev_y)
    own = jnp.where(first, endA, endB)
    last_copy.wait_recv()
    gt_out[...] = own + rY[...]

    for c in started:
        c.wait_send()


def build(nz, ny, nx, F, C, total_images):
    lfx, lbx = chain_lengths(nx)
    lfz, lbz = chain_lengths(nz)
    hz, xs = nz // 2, nx // 2
    tm = hz * nx * R
    nch = C // CH
    tw = 2 * F - F // 128 * 128
    f32, bf16 = jnp.float32, jnp.bfloat16

    def chain(n, shape, dtype):
        return pltpu.VMEM((max(n, 1),) + shape, dtype)

    smem = pltpu.SMEM
    scratch = [
        pltpu.VMEM((R, F), bf16),
        smem((C * nz * ny * nx * 2 // 128,), jnp.int32),
        smem((nz * ny,), jnp.int32),
        pltpu.VMEM((4, hz, nx, R, 2 * F), bf16),
        pltpu.VMEM((4, tw, tm), bf16),
        pltpu.VMEM((nch, 2 * F, 2 * CH), bf16),
        pltpu.VMEM((nch, 4, tm, 2 * CH), bf16),
        pltpu.VMEM((4, hz, nx, R, F), f32),
        pltpu.VMEM((nch, F, 2 * CH), f32),
        pltpu.VMEM((nch, F, CH), f32),
        pltpu.VMEM((4, tm, 128), jnp.int32),
        pltpu.VMEM((4, R, -(-F // 128) * 128), bf16),
        *[chain(n, (2, xs, R, F), WIRE_A) for n in (lfz, lbz, lfz, lbz)],
        *[chain(n, (2, hz, R, F), WIRE_B) for n in (lfx, lbx, lfx, lbx)],
        pltpu.VMEM((nx, R, F), f32),
        pltpu.VMEM((3, R, F), f32),
        pltpu.VMEM((2, hz, R, F), f32),
        pltpu.VMEM((4, R, F), WIRE_B),
        pltpu.VMEM((4, R, F), WIRE_B),
        pltpu.VMEM((7, R, F), f32),
        pltpu.VMEM((R, F), f32),
        pltpu.VMEM((R, F), f32),
        pltpu.SemaphoreType.DMA((140,)),
        pltpu.SemaphoreType.DMA((140,)),
        pltpu.SemaphoreType.DMA((nch + 3,)),
    ]
    vmem = pl.BlockSpec(memory_space=pltpu.VMEM)
    hbm = pl.BlockSpec(memory_space=pl.ANY)

    def body(images, texts, img_group, txt_group, temp, bias, loss_scale):
        gi, gt = pl.pallas_call(
            functools.partial(kernel, (nz, ny, nx, F, C, total_images)),
            out_shape=(pltpu.VMEM((F, C), f32), pltpu.VMEM((R, F), f32)),
            in_specs=[hbm] * 4 + [pl.BlockSpec(memory_space=pltpu.SMEM)] * 3,
            out_specs=(vmem, vmem),
            scratch_shapes=scratch,
            compiler_params=pltpu.CompilerParams(
                collective_id=0, has_side_effects=True, vmem_limit_bytes=56 * 1024 * 1024
            ),
        )(images.T, texts, img_group, txt_group, temp, bias, loss_scale)
        return gi.T, gt

    return body


def solution(mesh):
    body = build(NZ, NY, NX, 576, 1024, 131072)
    in_specs = (P("blk", "feat"), P("blk", "feat"), P(), P(), P(), P(), P())
    out_specs = (P("blk", "feat"), P("blk", "feat"))
    return jax.shard_map(body, mesh=mesh, in_specs=in_specs, out_specs=out_specs, check_vma=False)
```
